32 devices in a mesh: freq: 8 (over z, core), tm: 2 (over y), beam: 2 (over x).
Axes of the slice: x: 2, y: 2, z: 4, core: 2. Of those that a mesh axis runs over, the one named last changes fastest.
Arguments:
- raw_samples: bfloat16 [6144, 4096], P(('beam', 'tm'), 'freq'), parts along dimension 0, may hold values from -6 to 6
- filter_taps: bfloat16 [16, 4096], P(None, 'freq'), may hold values from -1.5 to 1.5
- dm_trials: int32 [256], replicated, may hold values from 0 to 1024, as said below
- channel_units: int32 [4096], replicated, may hold values from 0 to 512, as said below
Outputs:
- dm_power: float32 [4, 256, 256], P(('beam', 'tm'), 'freq'), parts along dimension 0
The draws below stay inside these ranges and needn't reach their ends.
There are 2 independent parts, one for each index of `beam`. The reference program is written for one: setup_inputs(seed, part) draws one part's arguments, and reference() takes and returns one part's arrays. A program takes and returns all parts, laid end to end along the dimension named above; an argument that names none is the same for every part. Nothing has to cross between parts.
Inputs may be any that keep to these rules, and one draw needn't show every extreme that they name: Trial d delays a channel of integer delay u by floor(dm_trials[d] * u / 1024) frames. `channel_units`: so that no dispersion delay exceeds 512 frames.
All inputs are finite; a program needn't handle non-finite values.
Results may differ from the reference program's by a relative error of at most 0.0072.
Values may be sent and summed in bfloat16 or wider, within the bound.
A program may use at most 64 MiB of HBM per device.

```python
import math
import jax
import jax.numpy as jnp
from jax import lax

CHANNELS = 4096
TAPS = 16
DFT_LEN = 2048
BINS = 256
SHARED = 512
DMS = 256
DM_STEPS = 1024
SEGS_DEV = 1
SEGMENTS = 2
FRAMES = 3072
N_FREQ = 8
N_TM = 2


def draw_dm_trials(key, part):
    values = jax.random.randint(jax.random.fold_in(key, 11), (DMS,), 0, DM_STEPS + 1, dtype=jnp.int32)
    marked = jax.random.randint(jax.random.fold_in(key, 12), (), 0, DMS, dtype=jnp.int32)
    return jnp.where(jnp.arange(DMS, dtype=jnp.int32) == marked, DM_STEPS, values).astype(jnp.int32)


def draw_channel_units(key, part):
    values = jax.random.randint(jax.random.fold_in(key, 21), (CHANNELS,), 0, SHARED + 1, dtype=jnp.int32)
    marked = jax.random.randint(jax.random.fold_in(key, 22), (), 0, CHANNELS, dtype=jnp.int32)
    return jnp.where(jnp.arange(CHANNELS, dtype=jnp.int32) == marked, SHARED, values).astype(jnp.int32)


def block_levels(own_key, shape, shards, smallest, largest):
    gain, own = 1.0, jax.random.fold_in(own_key, 6)
    for axis_at, blocks in shards:
        draws = jnp.exp(jax.random.uniform(jax.random.fold_in(own, axis_at), (blocks,), jnp.float32, smallest / len(shards), largest / len(shards)))
        gain = gain * jnp.repeat(draws, shape[axis_at] // blocks).reshape([-1 if axis == axis_at else 1 for axis in range(len(shape))])
    return gain


def centred(rng, shape, scale, limit, split=(), kind=jnp.bfloat16):
    gain = block_levels(rng, shape, split, -0.22, 0.18) if split else 1.0
    array = jax.random.normal(rng, shape, jnp.float32) * scale * gain
    return jnp.minimum(jnp.maximum(array, -limit), limit).astype(kind)


def setup_inputs(seed: int = 0, part: int = 0) -> dict:
    seeds = jax.random.split(jax.random.key(seed), 5)
    part_splits = jax.random.split(jax.random.fold_in(seeds[4], part), 5)
    raw_samples = centred(part_splits[0], (FRAMES, CHANNELS), 1.0, 6.0, ((0, 2), (1, 8)))
    filter_taps = centred(seeds[1], (TAPS, CHANNELS), TAPS ** -0.5, 1.5, ((1, 8),))
    dm_trials = draw_dm_trials(jax.random.fold_in(seeds[4], 71), part)
    channel_units = draw_channel_units(jax.random.fold_in(seeds[4], 71), part)
    return dict(raw_samples=raw_samples, filter_taps=filter_taps, dm_trials=dm_trials, channel_units=channel_units)


ramp_block = 32

def rounded(values):
    return lax.optimization_barrier(values.astype(jnp.bfloat16)).astype(jnp.float32)

def reference(raw_samples, filter_taps, dm_trials, channel_units):
    members = N_FREQ
    inner_len = CHANNELS // members
    step_len = DFT_LEN - SHARED
    own_len = SEGS_DEV * step_len
    frames = own_len + SHARED
    highest = lax.Precision.HIGHEST
    padded = jnp.pad(raw_samples.astype(jnp.float32), ((TAPS - 1, SHARED), (0, 0)))
    taps_wide = filter_taps.astype(jnp.float32)
    source = jnp.arange(members, dtype=jnp.int32)
    inner_ids = jnp.arange(inner_len, dtype=jnp.int32)
    phases_one = (inner_len * source[:, None, None] * source[None, None, :] + inner_ids[None, :, None] * source[None, None, :]) % CHANNELS
    angles_one = phases_one.astype(jnp.float32) * (2.0 * math.pi / CHANNELS)
    scale_one = 1.0 / math.sqrt(members)
    cos_one = rounded(jnp.cos(angles_one) * scale_one)
    sin_one = rounded(jnp.sin(angles_one) * scale_one)
    phases_two = inner_ids[:, None] * inner_ids[None, :] % inner_len
    angles_two = phases_two.astype(jnp.float32) * (2.0 * math.pi / inner_len)
    scale_two = 1.0 / math.sqrt(inner_len)
    cos_two = rounded(jnp.cos(angles_two) * scale_two)
    sin_two = rounded(jnp.sin(angles_two) * scale_two)
    bin_all = jnp.arange(BINS, dtype=jnp.int32)
    time_ids = jnp.arange(DFT_LEN, dtype=jnp.int32)
    phases_three = bin_all[:, None] * time_ids[None, :] % DFT_LEN
    angles_three = phases_three.astype(jnp.float32) * (2.0 * math.pi / DFT_LEN)
    scale_three = 1.0 / math.sqrt(DFT_LEN)
    cos_three = rounded(jnp.cos(angles_three) * scale_three)
    sin_three = rounded(jnp.sin(angles_three) * scale_three)

    def channelize(block_id):
        extended = lax.dynamic_slice_in_dim(padded, block_id * own_len, frames + TAPS - 1, 0)
        total = jnp.zeros((frames, CHANNELS), jnp.float32)
        for tap_id in range(TAPS):
            total = total + taps_wide[tap_id] * extended[TAPS - 1 - tap_id:TAPS - 1 - tap_id + frames]
        filtered = rounded(total)
        seg_reals = []
        seg_imags = []
        for seg_id in range(SEGS_DEV):
            piece = filtered[seg_id * step_len:seg_id * step_len + DFT_LEN]
            seg_reals.append(jnp.dot(cos_three, piece, precision=highest))
            seg_imags.append(-jnp.dot(sin_three, piece, precision=highest))
        seg_real = jnp.stack(seg_reals).reshape(SEGS_DEV * BINS, members, inner_len)
        seg_imag = jnp.stack(seg_imags).reshape(SEGS_DEV * BINS, members, inner_len)
        first_real = jnp.einsum('tfa,fak->tak', seg_real, cos_one, precision=highest) + jnp.einsum('tfa,fak->tak', seg_imag, sin_one, precision=highest)
        first_imag = jnp.einsum('tfa,fak->tak', seg_imag, cos_one, precision=highest) - jnp.einsum('tfa,fak->tak', seg_real, sin_one, precision=highest)
        chan_real = jnp.einsum('tak,am->tmk', first_real, cos_two, precision=highest) + jnp.einsum('tak,am->tmk', first_imag, sin_two, precision=highest)
        chan_imag = jnp.einsum('tak,am->tmk', first_imag, cos_two, precision=highest) - jnp.einsum('tak,am->tmk', first_real, sin_two, precision=highest)
        chan_real = rounded(chan_real).reshape(SEGS_DEV, BINS, CHANNELS)
        chan_imag = rounded(chan_imag).reshape(SEGS_DEV, BINS, CHANNELS)
        return jnp.stack([chan_real, chan_imag], axis=1)
    spectra = lax.map(channelize, jnp.arange(N_TM, dtype=jnp.int32))
    spectra = jnp.transpose(spectra, (3, 4, 0, 1, 2)).reshape(BINS, CHANNELS, SEGMENTS * 2)
    delays = dm_trials[:, None] * channel_units[None, :] // DM_STEPS
    norm = 1.0 / math.sqrt(CHANNELS)

    def ramp_piece(block_id):
        bin_ids = block_id * ramp_block + jnp.arange(ramp_block, dtype=jnp.int32)
        phases = bin_ids[:, None, None] * delays[None, :, :] % DFT_LEN
        angles = phases.astype(jnp.float32) * (2.0 * math.pi / DFT_LEN)
        cosine = rounded(jnp.cos(angles))
        sine = rounded(jnp.sin(angles))
        piece = lax.dynamic_slice_in_dim(spectra, block_id * ramp_block, ramp_block, 0)
        cos_part = jnp.einsum('bdc,bcx->bdx', cosine, piece, precision=highest)
        sin_part = jnp.einsum('bdc,bcx->bdx', sine, piece, precision=highest)
        return (cos_part, sin_part)
    cos_part, sin_part = lax.map(ramp_piece, jnp.arange(BINS // ramp_block, dtype=jnp.int32))
    cos_part = cos_part.reshape(BINS, DMS, SEGMENTS, 2)
    sin_part = sin_part.reshape(BINS, DMS, SEGMENTS, 2)
    real_part = (cos_part[..., 0] - sin_part[..., 1]) * norm
    imag_part = (sin_part[..., 0] + cos_part[..., 1]) * norm
    return jnp.transpose(real_part * real_part + imag_part * imag_part, (2, 1, 0))
```

```python
import math

import jax
import jax.numpy as jnp
import numpy as np
from jax import lax
from jax.experimental import pallas as pl
from jax.experimental.pallas import tpu as pltpu
from jax.sharding import PartitionSpec as P

TAPS = 16
DFT_LEN = 2048
BINS = 256
SHARED = 512
DMS = 256
DM_STEPS = 1024
CHANNELS = 4096
RADIX = 8
INNER = CHANNELS // RADIX
CHUNK = 16


def passed_along(value, axis, steps):
    count = lax.axis_size(axis)
    leading, last = (max(0, -steps), min(count, count - steps))
    return lax.ppermute(value, axis, [(source, source + steps) for source in range(leading, last)])


def tables():
    bins = np.arange(BINS)[:, None]
    angle = 2 * np.pi * (bins * np.arange(DFT_LEN)[None, :] % DFT_LEN) / DFT_LEN
    time = np.concatenate([np.cos(angle), -np.sin(angle)], 0) / math.sqrt(DFT_LEN)
    angle = 2 * np.pi * (bins * np.arange(TAPS)[None, :]) / DFT_LEN
    tap = np.concatenate([np.cos(angle), -np.sin(angle)], 0)
    ids = np.arange(INNER)
    angle = 2 * np.pi * (np.arange(RADIX)[:, None] * ids[None, :]) / CHANNELS
    twiddle = np.stack([np.cos(angle), -np.sin(angle)]) / math.sqrt(RADIX)
    angle = 2 * np.pi * (ids[:, None] * ids[None, :] % INNER) / INNER
    cosine, sine = np.cos(angle), np.sin(angle)
    channel = np.block([[cosine, -sine], [sine, cosine]]) / math.sqrt(INNER)
    return (
        jnp.asarray(time, jnp.bfloat16),
        jnp.asarray(tap, jnp.float32),
        jnp.asarray(twiddle, jnp.float32),
        jnp.asarray(channel, jnp.bfloat16),
    )


def unit_circle(phase):
    x = phase.astype(jnp.float32) * (2.0 * math.pi / DFT_LEN)
    y = x * x
    sine, cosine = jnp.full_like(y, -1 / 39916800), jnp.full_like(y, 1 / 479001600)
    for value in (1 / 362880, -1 / 5040, 1 / 120, -1 / 6, 1.0):
        sine = sine * y + value
    for value in (-1 / 3628800, 1 / 40320, -1 / 720, 1 / 24, -0.5, 1.0):
        cosine = cosine * y + value
    return cosine, sine * x


def fill_ramps(ramps, dms, first_bin):
    bins = ramps.shape[0]

    @pl.loop(0, SHARED // CHUNK)
    def _(step):
        row = pl.multiple_of(step * CHUNK, CHUNK)
        units = lax.broadcasted_iota(jnp.int32, (CHUNK, DMS), 0) + (row + 1)
        delays = (units * dms[...]) >> 10
        turn_cos, turn_sin = unit_circle(delays)
        phase = (delays * first_bin) & (DFT_LEN - 1)
        quarter = phase >> 9
        cosine, sine = unit_circle(phase & 511)
        odd = (quarter & 1) == 1
        swapped_cos = jnp.where(odd, -sine, cosine)
        swapped_sin = jnp.where(odd, cosine, sine)
        far = quarter >= 2
        cosine = jnp.where(far, -swapped_cos, swapped_cos)
        sine = jnp.where(far, -swapped_sin, swapped_sin)
        for at in range(bins):
            ramps[at, pl.ds(row, CHUNK), :] = cosine.astype(jnp.bfloat16)
            ramps[at, pl.ds(SHARED + row, CHUNK), :] = sine.astype(jnp.bfloat16)
            if at + 1 < bins:
                cosine, sine = (
                    cosine * turn_cos - sine * turn_sin,
                    sine * turn_cos + cosine * turn_sin,
                )


def dft(real, imag):
    count = len(real)
    if count == 1:
        return real, imag
    er, ei = dft(real[0::2], imag[0::2])
    odr, odi = dft(real[1::2], imag[1::2])
    half = count // 2
    outs = [None] * count
    for k in range(half):
        if k == 0:
            tr, ti = odr[k], odi[k]
        elif 4 * k == count:
            tr, ti = odi[k], -odr[k]
        else:
            c, s = math.cos(2 * math.pi * k / count), math.sin(2 * math.pi * k / count)
            tr, ti = odr[k] * c + odi[k] * s, odi[k] * c - odr[k] * s
        outs[k] = (er[k] + tr, ei[k] + ti)
        outs[k + half] = (er[k] - tr, ei[k] - ti)
    return [o[0] for o in outs], [o[1] for o in outs]


def channelize(held, twiddle, first):
    members, _, bins, width = held.shape
    per = members // RADIX
    for lane in range(INNER // 128):
        src, off = (lane * 128) // width, (lane * 128) % width
        real, imag = [], []
        for n2 in range(RADIX):
            real.append(held[n2 * per + src, 0, :, off : off + 128].astype(jnp.float32))
            imag.append(held[n2 * per + src, 1, :, off : off + 128].astype(jnp.float32))
        real, imag = dft(real, imag)
        cols = slice(lane * 128, lane * 128 + 128)
        cols_imag = slice(INNER + lane * 128, INNER + lane * 128 + 128)
        for k2 in range(RADIX):
            c, s = twiddle[0, k2 : k2 + 1, cols], twiddle[1, k2 : k2 + 1, cols]
            rows = slice(k2 * bins, k2 * bins + bins)
            first[rows, cols] = real[k2] * c - imag[k2] * s
            first[rows, cols_imag] = real[k2] * s + imag[k2] * c


def group_units(spectra, units, bins):
    grouped = jnp.zeros((2 * bins, SHARED), jnp.float32)
    whole = jnp.zeros((2 * bins, INNER), jnp.float32)
    ids = lax.broadcasted_iota(jnp.int32, (SHARED, INNER), 0) + 1
    for k2 in range(RADIX):
        part = spectra[k2 * bins : (k2 + 1) * bins]
        part = jnp.concatenate([part[:, :INNER], part[:, INNER:]], 0)
        part = part.astype(jnp.bfloat16)
        whole += part.astype(jnp.float32)
        same = (ids == units[k2 : k2 + 1, :]).astype(jnp.float32).astype(jnp.bfloat16)
        grouped += lax.dot_general(
            part, same, (((1,), (1,)), ((), ())), preferred_element_type=jnp.float32
        )
    rest = jnp.sum(whole, 1, keepdims=True) - jnp.sum(grouped, 1, keepdims=True)
    return grouped, rest


def tail_kernel(held, units, dms, twiddle, channel, power, ramps, first):
    bins = power.shape[0]
    fill_ramps(ramps, dms, lax.axis_index("freq") * bins)
    channelize(held, twiddle, first)
    spectra = jnp.dot(
        first[...].astype(jnp.bfloat16), channel[...], preferred_element_type=jnp.float32
    )
    grouped, rest = group_units(spectra, units, bins)
    real, imag = grouped[:bins], grouped[bins:]
    upper = jnp.concatenate([real, -imag], 1)
    lower = jnp.concatenate([imag, real], 1)
    for at in range(bins):
        left = jnp.concatenate([upper[at : at + 1], lower[at : at + 1]], 0)
        total = jnp.dot(
            left.astype(jnp.bfloat16), ramps[at], preferred_element_type=jnp.float32
        )
        re = total[0:1] + rest[at : at + 1]
        im = total[1:2] + rest[bins + at : bins + at + 1]
        power[at : at + 1, :] = (re * re + im * im) * (1.0 / CHANNELS)


def body(raw_samples, filter_taps, dm_trials, channel_units):
    members = lax.axis_size("freq")
    own_len, width = raw_samples.shape
    bins = BINS // members
    time, tap, twiddle, channel = tables()
    highest = lax.Precision.HIGHEST
    earlier = passed_along(raw_samples[own_len - (TAPS - 1) :], "tm", 1)
    later = passed_along(raw_samples[:SHARED], "tm", -1)
    spec = jnp.dot(
        time, jnp.concatenate([raw_samples, later], 0), preferred_element_type=jnp.float32
    )
    taps = filter_taps.astype(jnp.float32)
    edge = (earlier.astype(jnp.float32) - later[SHARED - (TAPS - 1) :].astype(jnp.float32))[::-1]
    padded = jnp.concatenate([taps, jnp.zeros_like(taps)], 0)
    fringe = jnp.zeros_like(taps)
    for e in range(1, TAPS):
        fringe = fringe + padded[e : e + TAPS] * edge[e - 1 : e]
    gain = jnp.dot(tap, taps, precision=highest)
    extra = jnp.dot(tap, fringe * (1.0 / math.sqrt(DFT_LEN)), precision=highest)
    sr, si, gr, gi = spec[:BINS], spec[BINS:], gain[:BINS], gain[BINS:]
    seg = jnp.stack([sr * gr - si * gi + extra[:BINS], sr * gi + si * gr + extra[BINS:]])
    seg = seg.astype(jnp.bfloat16).reshape(2, members, bins, width).transpose(1, 0, 2, 3)
    held = lax.all_to_all(seg, "freq", split_axis=0, concat_axis=0, tiled=True)
    units = channel_units.reshape(INNER, RADIX).T
    vmem = pl.BlockSpec(memory_space=pltpu.VMEM)
    power = pl.pallas_call(
        tail_kernel,
        out_shape=jax.ShapeDtypeStruct((bins, DMS), jnp.float32),
        in_specs=[vmem] * 5,
        out_specs=vmem,
        scratch_shapes=[
            pltpu.VMEM((bins, 2 * SHARED, DMS), jnp.bfloat16),
            pltpu.VMEM((RADIX * bins, 2 * INNER), jnp.float32),
        ],
        compiler_params=pltpu.CompilerParams(vmem_limit_bytes=48 * 2**20),
    )(held, units, dm_trials.reshape(1, DMS), twiddle, channel)
    power = lax.all_to_all(power, "freq", split_axis=1, concat_axis=0, tiled=True)
    return power.T[None]


def solution(mesh):
    in_specs = (P(("beam", "tm"), "freq"), P(None, "freq"), P(), P())
    out_specs = P(("beam", "tm"), "freq", None)
    return jax.shard_map(body, mesh=mesh, in_specs=in_specs, out_specs=out_specs, check_vma=False)
```

```python
import functools
import math

import jax
import jax.numpy as jnp
import numpy as np
from jax import lax
from jax.experimental import pallas as pl
from jax.experimental.pallas import tpu as pltpu
from jax.sharding import PartitionSpec as P

TAPS = 16
DFT_LEN = 2048
BINS = 256
SHARED = 512
DMS = 256
DM_STEPS = 1024
CHANNELS = 4096
RADIX = 8
INNER = CHANNELS // RADIX
CHUNK = 16


def tables():
    bins = np.arange(BINS)[:, None]
    angle = 2 * np.pi * (bins * np.arange(DFT_LEN)[None, :] % DFT_LEN) / DFT_LEN
    time = np.concatenate([np.cos(angle), -np.sin(angle)], 0) / math.sqrt(DFT_LEN)
    angle = 2 * np.pi * (bins * np.arange(TAPS)[None, :]) / DFT_LEN
    tap = np.concatenate([np.cos(angle), -np.sin(angle)], 0)
    ids = np.arange(INNER)
    angle = 2 * np.pi * (np.arange(RADIX)[:, None] * ids[None, :]) / CHANNELS
    twiddle = np.stack([np.cos(angle), -np.sin(angle)]) / math.sqrt(RADIX)
    angle = 2 * np.pi * (ids[:, None] * ids[None, :] % INNER) / INNER
    cosine, sine = np.cos(angle), np.sin(angle)
    channel = np.block([[cosine, -sine], [sine, cosine]]) / math.sqrt(INNER)
    return (
        jnp.asarray(time, jnp.bfloat16),
        jnp.asarray(tap, jnp.float32),
        jnp.asarray(twiddle, jnp.float32),
        jnp.asarray(channel, jnp.bfloat16),
    )


def unit_circle(phase):
    x = phase.astype(jnp.float32) * (2.0 * math.pi / DFT_LEN)
    y = x * x
    sine, cosine = jnp.full_like(y, -1 / 39916800), jnp.full_like(y, 1 / 479001600)
    for value in (1 / 362880, -1 / 5040, 1 / 120, -1 / 6, 1.0):
        sine = sine * y + value
    for value in (-1 / 3628800, 1 / 40320, -1 / 720, 1 / 24, -0.5, 1.0):
        cosine = cosine * y + value
    return cosine, sine * x


def fill_ramps(ramps, dms, first_bin):
    bins = ramps.shape[0]

    @pl.loop(0, SHARED // CHUNK)
    def _(step):
        row = pl.multiple_of(step * CHUNK, CHUNK)
        units = lax.broadcasted_iota(jnp.int32, (CHUNK, DMS), 0) + (row + 1)
        delays = (units * dms[...]) >> 10
        turn_cos, turn_sin = unit_circle(delays)
        phase = (delays * first_bin) & (DFT_LEN - 1)
        quarter = phase >> 9
        cosine, sine = unit_circle(phase & 511)
        odd = (quarter & 1) == 1
        swapped_cos = jnp.where(odd, -sine, cosine)
        swapped_sin = jnp.where(odd, cosine, sine)
        far = quarter >= 2
        cosine = jnp.where(far, -swapped_cos, swapped_cos)
        sine = jnp.where(far, -swapped_sin, swapped_sin)
        for at in range(bins):
            ramps[at, pl.ds(row, CHUNK), :] = cosine.astype(jnp.bfloat16)
            ramps[at, pl.ds(SHARED + row, CHUNK), :] = sine.astype(jnp.bfloat16)
            if at + 1 < bins:
                cosine, sine = (
                    cosine * turn_cos - sine * turn_sin,
                    sine * turn_cos + cosine * turn_sin,
                )


def dft(real, imag):
    count = len(real)
    if count == 1:
        return real, imag
    er, ei = dft(real[0::2], imag[0::2])
    odr, odi = dft(real[1::2], imag[1::2])
    half = count // 2
    outs = [None] * count
    for k in range(half):
        if k == 0:
            tr, ti = odr[k], odi[k]
        elif 4 * k == count:
            tr, ti = odi[k], -odr[k]
        else:
            c, s = math.cos(2 * math.pi * k / count), math.sin(2 * math.pi * k / count)
            tr, ti = odr[k] * c + odi[k] * s, odi[k] * c - odr[k] * s
        outs[k] = (er[k] + tr, ei[k] + ti)
        outs[k + half] = (er[k] - tr, ei[k] - ti)
    return [o[0] for o in outs], [o[1] for o in outs]


def channelize(held, twiddle, first):
    members, _, bins, width = held.shape
    per = members // RADIX
    for lane in range(INNER // 128):
        src, off = (lane * 128) // width, (lane * 128) % width
        real, imag = [], []
        for n2 in range(RADIX):
            real.append(held[n2 * per + src, 0, :, off : off + 128].astype(jnp.float32))
            imag.append(held[n2 * per + src, 1, :, off : off + 128].astype(jnp.float32))
        real, imag = dft(real, imag)
        cols = slice(lane * 128, lane * 128 + 128)
        cols_imag = slice(INNER + lane * 128, INNER + lane * 128 + 128)
        for k2 in range(RADIX):
            c, s = twiddle[0, k2 : k2 + 1, cols], twiddle[1, k2 : k2 + 1, cols]
            rows = slice(k2 * bins, k2 * bins + bins)
            first[rows, cols] = real[k2] * c - imag[k2] * s
            first[rows, cols_imag] = real[k2] * s + imag[k2] * c


def fill_matches(matches, units):
    ids = lax.broadcasted_iota(jnp.int32, (SHARED, INNER), 0) + 1

    @pl.loop(0, RADIX)
    def _(k2):
        same = (ids == units[k2]).astype(jnp.float32)
        matches[k2] = same.astype(jnp.bfloat16)


def group_units(spectra, matches, bins):
    grouped = jnp.zeros((2 * bins, SHARED), jnp.float32)
    whole = jnp.zeros((2 * bins, INNER), jnp.float32)
    for k2 in range(RADIX):
        part = spectra[k2 * bins : (k2 + 1) * bins]
        part = jnp.concatenate([part[:, :INNER], part[:, INNER:]], 0)
        part = part.astype(jnp.bfloat16)
        whole += part.astype(jnp.float32)
        grouped += lax.dot_general(
            part, matches[k2], (((1,), (1,)), ((), ())), preferred_element_type=jnp.float32
        )
    rest = jnp.sum(whole, 1, keepdims=True) - jnp.sum(grouped, 1, keepdims=True)
    return grouped, rest


def partner_order(members):
    return sorted(range(1, members), key=lambda o: abs(o - members // 2))


def kernel(
    members, segments,
    raw, time_hbm, channel_hbm, filter_taps, units, dms, tap, twiddle,
    out,
    own, time, channel, later, tail, padded, spec, gain, extra, outgoing, held,
    ramps, matches, first, power_out, power_in,
    local_sem, halo_send, halo_recv, seg_send, seg_recv, pow_send, pow_recv,
):
    me = lax.axis_index("freq")
    seg = lax.axis_index("tm")
    own_len, width = own.shape
    bins = BINS // members
    kept = DMS // members
    loads = [
        pltpu.make_async_copy(raw, own, local_sem.at[0]),
        pltpu.make_async_copy(time_hbm, time, local_sem.at[1]),
        pltpu.make_async_copy(channel_hbm, channel, local_sem.at[2]),
    ]
    for load in loads:
        load.start()

    barrier = pltpu.get_barrier_semaphore()
    order = partner_order(members)
    for o in order:
        pl.semaphore_signal(
            barrier, inc=1, device_id={"freq": lax.rem(me + o, members)},
            device_id_type=pl.DeviceIdType.MESH,
        )

    @pl.when(seg > 0)
    def _():
        pl.semaphore_signal(
            barrier, inc=1, device_id={"tm": seg - 1}, device_id_type=pl.DeviceIdType.MESH
        )

    @pl.when(seg < segments - 1)
    def _():
        pl.semaphore_signal(
            barrier, inc=1, device_id={"tm": seg + 1}, device_id_type=pl.DeviceIdType.MESH
        )

    pl.semaphore_wait(
        barrier, members - 1 + jnp.minimum(seg, 1) + jnp.minimum(segments - 1 - seg, 1)
    )

    def back_copy():
        return pltpu.make_async_remote_copy(
            src_ref=raw.at[pl.ds(0, SHARED)], dst_ref=later,
            send_sem=halo_send.at[0], recv_sem=halo_recv.at[0],
            device_id={"tm": seg - 1}, device_id_type=pl.DeviceIdType.MESH,
        )

    def forward_copy():
        return pltpu.make_async_remote_copy(
            src_ref=raw.at[pl.ds(own_len - TAPS, TAPS)], dst_ref=tail,
            send_sem=halo_send.at[1], recv_sem=halo_recv.at[1],
            device_id={"tm": seg + 1}, device_id_type=pl.DeviceIdType.MESH,
        )

    @pl.when(seg > 0)
    def _():
        back_copy().start()

    @pl.when(seg == 0)
    def _():
        tail[...] = jnp.zeros_like(tail)

    @pl.when(seg < segments - 1)
    def _():
        forward_copy().start()

    @pl.when(seg == segments - 1)
    def _():
        later[...] = jnp.zeros_like(later)

    for load in loads:
        load.wait()
    taps = filter_taps[...].astype(jnp.float32)
    padded[0:TAPS, :] = taps
    padded[TAPS:, :] = jnp.zeros_like(taps)
    gain[...] = jnp.dot(
        tap[...], taps, precision=lax.Precision.HIGHEST, preferred_element_type=jnp.float32
    )
    spec[...] = jnp.dot(
        time[:, 0:own_len], own[...], preferred_element_type=jnp.float32
    )
    fill_ramps(ramps, dms, me * bins)

    @pl.when(seg > 0)
    def _():
        forward_copy().wait_recv()

    @pl.when(seg < segments - 1)
    def _():
        back_copy().wait_recv()

    edge = tail[...].astype(jnp.float32) - later[SHARED - TAPS :, :].astype(jnp.float32)
    fringe = jnp.zeros_like(taps)
    for e in range(1, TAPS):
        fringe = fringe + padded[e : e + TAPS, :] * edge[TAPS - e : TAPS - e + 1]
    extra[...] = jnp.dot(
        tap[...], fringe * (1.0 / math.sqrt(DFT_LEN)),
        precision=lax.Precision.HIGHEST, preferred_element_type=jnp.float32,
    )
    spec[...] += jnp.dot(
        time[:, own_len:], later[...], preferred_element_type=jnp.float32
    )

    def seg_copy(slot, target):
        return pltpu.make_async_remote_copy(
            src_ref=outgoing.at[target], dst_ref=held.at[slot],
            send_sem=seg_send.at[target], recv_sem=seg_recv.at[slot],
            device_id={"freq": target}, device_id_type=pl.DeviceIdType.MESH,
        )

    def block(target):
        row = pl.multiple_of(target * bins, bins)
        up, low = pl.ds(row, bins), pl.ds(BINS + row, bins)
        sr, si, gr, gi = spec[up, :], spec[low, :], gain[up, :], gain[low, :]
        real = sr * gr - si * gi + extra[up, :]
        imag = sr * gi + si * gr + extra[low, :]
        return real.astype(jnp.bfloat16), imag.astype(jnp.bfloat16)

    for o in order:
        target = lax.rem(me + o, members)
        outgoing[target, 0], outgoing[target, 1] = block(target)
        seg_copy(me, target).start()
    held[me, 0], held[me, 1] = block(me)
    fill_matches(matches, units)

    for o in order:
        source = lax.rem(me + o, members)
        seg_copy(source, source).wait_recv()
    channelize(held, twiddle, first)
    spectra = jnp.dot(
        first[...].astype(jnp.bfloat16), channel[...], preferred_element_type=jnp.float32
    )
    grouped, rest = group_units(spectra, matches, bins)
    real, imag = grouped[:bins], grouped[bins:]
    upper = jnp.concatenate([real, -imag], 1)
    lower = jnp.concatenate([imag, real], 1)
    rows = []
    for at in range(bins):
        left = jnp.concatenate([upper[at : at + 1], lower[at : at + 1]], 0)
        total = jnp.dot(
            left.astype(jnp.bfloat16), ramps[at], preferred_element_type=jnp.float32
        )
        re = total[0:1] + rest[at : at + 1]
        im = total[1:2] + rest[bins + at : bins + at + 1]
        rows.append((re * re + im * im) * (1.0 / CHANNELS))
    turned = jnp.concatenate(rows, 0).T
    for target in range(members):
        power_out[target] = turned[target * kept : (target + 1) * kept]

    def power_copy(slot, target):
        return pltpu.make_async_remote_copy(
            src_ref=power_out.at[target], dst_ref=power_in.at[slot],
            send_sem=pow_send.at[target], recv_sem=pow_recv.at[slot],
            device_id={"freq": target}, device_id_type=pl.DeviceIdType.MESH,
        )

    for o in order:
        power_copy(me, lax.rem(me + o, members)).start()
    power_in[me] = power_out[me]
    for o in order:
        target = lax.rem(me + o, members)
        power_copy(target, target).wait_recv()
    out[...] = jnp.concatenate([power_in[source] for source in range(members)], 1)
    for o in order:
        target = lax.rem(me + o, members)
        seg_copy(target, target).wait_send()
        power_copy(target, target).wait_send()

    @pl.when(seg > 0)
    def _():
        back_copy().wait_send()

    @pl.when(seg < segments - 1)
    def _():
        forward_copy().wait_send()


def body(raw_samples, filter_taps, dm_trials, channel_units):
    members = lax.axis_size("freq")
    own_len, width = raw_samples.shape
    bins, kept = BINS // members, DMS // members
    time, tap, twiddle, channel = tables()
    units = channel_units.reshape(INNER, RADIX).T.reshape(RADIX, 1, INNER)
    vmem = pl.BlockSpec(memory_space=pltpu.VMEM)
    anywhere = pl.BlockSpec(memory_space=pl.ANY)
    dma = pltpu.SemaphoreType.DMA
    power = pl.pallas_call(
        functools.partial(kernel, members, lax.axis_size("tm")),
        out_shape=jax.ShapeDtypeStruct((kept, BINS), jnp.float32),
        in_specs=[anywhere] * 3 + [vmem] * 5,
        out_specs=vmem,
        scratch_shapes=[
            pltpu.VMEM((own_len, width), jnp.bfloat16),
            pltpu.VMEM(time.shape, jnp.bfloat16),
            pltpu.VMEM(channel.shape, jnp.bfloat16),
            pltpu.VMEM((SHARED, width), jnp.bfloat16),
            pltpu.VMEM((TAPS, width), jnp.bfloat16),
            pltpu.VMEM((2 * TAPS, width), jnp.float32),
            pltpu.VMEM((2 * BINS, width), jnp.float32),
            pltpu.VMEM((2 * BINS, width), jnp.float32),
            pltpu.VMEM((2 * BINS, width), jnp.float32),
            pltpu.VMEM((members, 2, bins, width), jnp.bfloat16),
            pltpu.VMEM((members, 2, bins, width), jnp.bfloat16),
            pltpu.VMEM((bins, 2 * SHARED, DMS), jnp.bfloat16),
            pltpu.VMEM((RADIX, SHARED, INNER), jnp.bfloat16),
            pltpu.VMEM((RADIX * bins, 2 * INNER), jnp.float32),
            pltpu.VMEM((members, kept, bins), jnp.float32),
            pltpu.VMEM((members, kept, bins), jnp.float32),
            dma((3,)), dma((2,)), dma((2,)),
            dma((members,)), dma((members,)), dma((members,)), dma((members,)),
        ],
        compiler_params=pltpu.CompilerParams(
            vmem_limit_bytes=56 * 2**20, collective_id=0, has_side_effects=True
        ),
    )(raw_samples, time, channel, filter_taps, units, dm_trials.reshape(1, DMS), tap, twiddle)
    return power[None]


def solution(mesh):
    in_specs = (P(("beam", "tm"), "freq"), P(None, "freq"), P(), P())
    out_specs = P(("beam", "tm"), "freq", None)
    return jax.shard_map(body, mesh=mesh, in_specs=in_specs, out_specs=out_specs, check_vma=False)
```

```python
import functools
import math

import jax
import jax.numpy as jnp
import numpy as np
from jax import lax
from jax.experimental import pallas as pl
from jax.experimental.pallas import tpu as pltpu
from jax.sharding import PartitionSpec as P

TAPS = 16
DFT_LEN = 2048
BINS = 256
SHARED = 512
DMS = 256
DM_STEPS = 1024
CHANNELS = 4096
RADIX = 8
INNER = CHANNELS // RADIX
CHUNK = 16
LANES = 128


def tables():
    bins = np.arange(BINS)[:, None]
    angle = 2 * np.pi * (bins * np.arange(DFT_LEN)[None, :] % DFT_LEN) / DFT_LEN
    time = np.concatenate([np.cos(angle), -np.sin(angle)], 0) / math.sqrt(DFT_LEN)
    angle = 2 * np.pi * (bins * np.arange(TAPS)[None, :]) / DFT_LEN
    tap = np.concatenate([np.cos(angle), -np.sin(angle)], 0)
    ids = np.arange(INNER)
    angle = 2 * np.pi * (np.arange(RADIX)[:, None] * ids[None, :]) / CHANNELS
    twiddle = np.stack([np.cos(angle), -np.sin(angle)]) / math.sqrt(RADIX)
    angle = 2 * np.pi * (ids[:, None] * ids[None, :] % INNER) / INNER
    cosine, sine = np.cos(angle), np.sin(angle)
    channel = np.block([[cosine, -sine], [sine, cosine]]) / math.sqrt(INNER)
    return (
        jnp.asarray(time, jnp.bfloat16),
        jnp.asarray(tap, jnp.float32),
        jnp.asarray(twiddle, jnp.float32),
        jnp.asarray(channel, jnp.bfloat16),
    )


def unit_circle(phase):
    x = phase.astype(jnp.float32) * (2.0 * math.pi / DFT_LEN)
    y = x * x
    sine, cosine = jnp.full_like(y, -1 / 39916800), jnp.full_like(y, 1 / 479001600)
    for value in (1 / 362880, -1 / 5040, 1 / 120, -1 / 6, 1.0):
        sine = sine * y + value
    for value in (-1 / 3628800, 1 / 40320, -1 / 720, 1 / 24, -0.5, 1.0):
        cosine = cosine * y + value
    return cosine, sine * x


def fill_ramps(ramps, dms, first_bin, start, stop):
    bins = ramps.shape[0]

    @pl.loop(start, stop)
    def _(step):
        row = pl.multiple_of(step * CHUNK, CHUNK)
        units = lax.broadcasted_iota(jnp.int32, (CHUNK, DMS), 0) + (row + 1)
        delays = (units * dms[...]) >> 10
        turn_cos, turn_sin = unit_circle(delays)
        phase = (delays * first_bin) & (DFT_LEN - 1)
        quarter = phase >> 9
        cosine, sine = unit_circle(phase & 511)
        odd = (quarter & 1) == 1
        swapped_cos = jnp.where(odd, -sine, cosine)
        swapped_sin = jnp.where(odd, cosine, sine)
        far = quarter >= 2
        cosine = jnp.where(far, -swapped_cos, swapped_cos)
        sine = jnp.where(far, -swapped_sin, swapped_sin)
        for at in range(bins):
            ramps[at, pl.ds(row, CHUNK), :] = cosine.astype(jnp.bfloat16)
            ramps[at, pl.ds(SHARED + row, CHUNK), :] = sine.astype(jnp.bfloat16)
            if at + 1 < bins:
                cosine, sine = (
                    cosine * turn_cos - sine * turn_sin,
                    sine * turn_cos + cosine * turn_sin,
                )


def dft(real, imag):
    count = len(real)
    if count == 1:
        return real, imag
    er, ei = dft(real[0::2], imag[0::2])
    odr, odi = dft(real[1::2], imag[1::2])
    half = count // 2
    outs = [None] * count
    for k in range(half):
        if k == 0:
            tr, ti = odr[k], odi[k]
        elif 4 * k == count:
            tr, ti = odi[k], -odr[k]
        else:
            c, s = math.cos(2 * math.pi * k / count), math.sin(2 * math.pi * k / count)
            tr, ti = odr[k] * c + odi[k] * s, odi[k] * c - odr[k] * s
        outs[k] = (er[k] + tr, ei[k] + ti)
        outs[k + half] = (er[k] - tr, ei[k] - ti)
    return [o[0] for o in outs], [o[1] for o in outs]


def channelize(held, twiddle, first, slab):
    slabs, members, _, bins, _ = held.shape
    per = members // RADIX
    for src in range(per):
        lane = src * slabs + slab
        real, imag = [], []
        for n2 in range(RADIX):
            real.append(held[slab, n2 * per + src, 0].astype(jnp.float32))
            imag.append(held[slab, n2 * per + src, 1].astype(jnp.float32))
        real, imag = dft(real, imag)
        cols = slice(lane * 128, lane * 128 + 128)
        cols_imag = slice(INNER + lane * 128, INNER + lane * 128 + 128)
        for k2 in range(RADIX):
            c, s = twiddle[0, k2 : k2 + 1, cols], twiddle[1, k2 : k2 + 1, cols]
            rows = slice(k2 * bins, k2 * bins + bins)
            first[rows, cols] = real[k2] * c - imag[k2] * s
            first[rows, cols_imag] = real[k2] * s + imag[k2] * c


def fill_matches(matches, units):
    ids = lax.broadcasted_iota(jnp.int32, (SHARED, INNER), 0) + 1

    @pl.loop(0, RADIX)
    def _(k2):
        same = (ids == units[k2]).astype(jnp.float32)
        matches[k2] = same.astype(jnp.bfloat16)


def group_units(spectra, matches, bins):
    grouped = jnp.zeros((2 * bins, SHARED), jnp.float32)
    whole = jnp.zeros((2 * bins, INNER), jnp.float32)
    for k2 in range(RADIX):
        part = spectra[k2 * bins : (k2 + 1) * bins]
        part = jnp.concatenate([part[:, :INNER], part[:, INNER:]], 0)
        part = part.astype(jnp.bfloat16)
        whole += part.astype(jnp.float32)
        grouped += lax.dot_general(
            part, matches[k2], (((1,), (1,)), ((), ())), preferred_element_type=jnp.float32
        )
    rest = jnp.sum(whole, 1, keepdims=True) - jnp.sum(grouped, 1, keepdims=True)
    return grouped, rest


def partner_order(members):
    return sorted(range(1, members), key=lambda o: abs(o - members // 2))


def kernel(
    members, segments,
    raw, time_hbm, channel_hbm, filter_taps, units, dms, tap, twiddle,
    out,
    own, time, channel, later, tail, padded, spec, gain, extra, outgoing, held,
    ramps, matches, first, power_out, power_in,
    local_sem, halo_send, halo_recv, seg_send, seg_recv, pow_send, pow_recv,
):
    me = lax.axis_index("freq")
    seg = lax.axis_index("tm")
    own_len, width = own.shape
    bins = BINS // members
    kept = DMS // members
    loads = [
        pltpu.make_async_copy(raw, own, local_sem.at[0]),
        pltpu.make_async_copy(time_hbm, time, local_sem.at[1]),
        pltpu.make_async_copy(channel_hbm, channel, local_sem.at[2]),
    ]
    for load in loads:
        load.start()

    barrier = pltpu.get_barrier_semaphore()
    order = partner_order(members)
    for o in order:
        pl.semaphore_signal(
            barrier, inc=1, device_id={"freq": lax.rem(me + o, members)},
            device_id_type=pl.DeviceIdType.MESH,
        )

    @pl.when(seg > 0)
    def _():
        pl.semaphore_signal(
            barrier, inc=1, device_id={"tm": seg - 1}, device_id_type=pl.DeviceIdType.MESH
        )

    @pl.when(seg < segments - 1)
    def _():
        pl.semaphore_signal(
            barrier, inc=1, device_id={"tm": seg + 1}, device_id_type=pl.DeviceIdType.MESH
        )

    pl.semaphore_wait(
        barrier, members - 1 + jnp.minimum(seg, 1) + jnp.minimum(segments - 1 - seg, 1)
    )

    slabs = width // LANES

    def back_copy(slab):
        return pltpu.make_async_remote_copy(
            src_ref=raw.at[pl.ds(0, SHARED), pl.ds(slab * LANES, LANES)],
            dst_ref=later.at[slab],
            send_sem=halo_send.at[1 + slab], recv_sem=halo_recv.at[1 + slab],
            device_id={"tm": seg - 1}, device_id_type=pl.DeviceIdType.MESH,
        )

    def forward_copy():
        return pltpu.make_async_remote_copy(
            src_ref=raw.at[pl.ds(own_len - TAPS, TAPS)], dst_ref=tail,
            send_sem=halo_send.at[0], recv_sem=halo_recv.at[0],
            device_id={"tm": seg + 1}, device_id_type=pl.DeviceIdType.MESH,
        )

    @pl.when(seg > 0)
    def _():
        for slab in range(slabs):
            back_copy(slab).start()

    @pl.when(seg == 0)
    def _():
        tail[...] = jnp.zeros_like(tail)

    @pl.when(seg < segments - 1)
    def _():
        forward_copy().start()

    @pl.when(seg == segments - 1)
    def _():
        later[...] = jnp.zeros_like(later)

    for load in loads:
        load.wait()
    taps = filter_taps[...].astype(jnp.float32)
    padded[0:TAPS, :] = taps
    padded[TAPS:, :] = jnp.zeros_like(taps)
    gain[...] = jnp.dot(
        tap[...], taps, precision=lax.Precision.HIGHEST, preferred_element_type=jnp.float32
    )
    spec[...] = jnp.dot(
        time[:, 0:own_len], own[...], preferred_element_type=jnp.float32
    )

    @pl.when(seg > 0)
    def _():
        forward_copy().wait_recv()

    def seg_copy(slab, slot, target):
        return pltpu.make_async_remote_copy(
            src_ref=outgoing.at[slab, target], dst_ref=held.at[slab, slot],
            send_sem=seg_send.at[slab, target], recv_sem=seg_recv.at[slab, slot],
            device_id={"freq": target}, device_id_type=pl.DeviceIdType.MESH,
        )

    def block(target, cols):
        row = pl.multiple_of(target * bins, bins)
        up, low = pl.ds(row, bins), pl.ds(BINS + row, bins)
        sr, si, gr, gi = spec[up, cols], spec[low, cols], gain[up, cols], gain[low, cols]
        real = sr * gr - si * gi + extra[up, :]
        imag = sr * gi + si * gr + extra[low, :]
        return real.astype(jnp.bfloat16), imag.astype(jnp.bfloat16)

    steps = SHARED // CHUNK // slabs
    for slab in range(slabs):
        cols = slice(slab * LANES, (slab + 1) * LANES)

        @pl.when(seg < segments - 1)
        def _():
            back_copy(slab).wait_recv()

        edge = tail[:, cols].astype(jnp.float32)
        edge = edge - later[slab, SHARED - TAPS :, :].astype(jnp.float32)
        fringe = jnp.zeros_like(edge)
        for e in range(1, TAPS):
            fringe = fringe + padded[e : e + TAPS, cols] * edge[TAPS - e : TAPS - e + 1]
        extra[...] = jnp.dot(
            tap[...], fringe * (1.0 / math.sqrt(DFT_LEN)),
            precision=lax.Precision.HIGHEST, preferred_element_type=jnp.float32,
        )
        spec[:, cols] += jnp.dot(
            time[:, own_len:], later[slab], preferred_element_type=jnp.float32
        )
        for o in order:
            target = lax.rem(me + o, members)
            outgoing[slab, target, 0], outgoing[slab, target, 1] = block(target, cols)
            seg_copy(slab, me, target).start()
        held[slab, me, 0], held[slab, me, 1] = block(me, cols)
        fill_ramps(ramps, dms, me * bins, slab * steps, (slab + 1) * steps)
    fill_matches(matches, units)

    for slab in range(slabs):
        for o in order:
            source = lax.rem(me + o, members)
            seg_copy(slab, source, source).wait_recv()
        channelize(held, twiddle, first, slab)
    spectra = jnp.dot(
        first[...].astype(jnp.bfloat16), channel[...], preferred_element_type=jnp.float32
    )
    grouped, rest = group_units(spectra, matches, bins)
    real, imag = grouped[:bins], grouped[bins:]
    upper = jnp.concatenate([real, -imag], 1)
    lower = jnp.concatenate([imag, real], 1)
    rows = []
    for at in range(bins):
        left = jnp.concatenate([upper[at : at + 1], lower[at : at + 1]], 0)
        total = jnp.dot(
            left.astype(jnp.bfloat16), ramps[at], preferred_element_type=jnp.float32
        )
        re = total[0:1] + rest[at : at + 1]
        im = total[1:2] + rest[bins + at : bins + at + 1]
        rows.append((re * re + im * im) * (1.0 / CHANNELS))
    turned = jnp.concatenate(rows, 0).T
    for target in range(members):
        power_out[target] = turned[target * kept : (target + 1) * kept]

    def power_copy(slot, target):
        return pltpu.make_async_remote_copy(
            src_ref=power_out.at[target], dst_ref=power_in.at[slot],
            send_sem=pow_send.at[target], recv_sem=pow_recv.at[slot],
            device_id={"freq": target}, device_id_type=pl.DeviceIdType.MESH,
        )

    for o in order:
        power_copy(me, lax.rem(me + o, members)).start()
    power_in[me] = power_out[me]
    for o in order:
        target = lax.rem(me + o, members)
        power_copy(target, target).wait_recv()
    out[...] = jnp.concatenate([power_in[source] for source in range(members)], 1)
    for o in order:
        target = lax.rem(me + o, members)
        for slab in range(slabs):
            seg_copy(slab, target, target).wait_send()
        power_copy(target, target).wait_send()

    @pl.when(seg > 0)
    def _():
        for slab in range(slabs):
            back_copy(slab).wait_send()

    @pl.when(seg < segments - 1)
    def _():
        forward_copy().wait_send()


def body(raw_samples, filter_taps, dm_trials, channel_units):
    members = lax.axis_size("freq")
    own_len, width = raw_samples.shape
    bins, kept, slabs = BINS // members, DMS // members, width // LANES
    time, tap, twiddle, channel = tables()
    units = channel_units.reshape(INNER, RADIX).T.reshape(RADIX, 1, INNER)
    vmem = pl.BlockSpec(memory_space=pltpu.VMEM)
    anywhere = pl.BlockSpec(memory_space=pl.ANY)
    dma = pltpu.SemaphoreType.DMA
    power = pl.pallas_call(
        functools.partial(kernel, members, lax.axis_size("tm")),
        out_shape=jax.ShapeDtypeStruct((kept, BINS), jnp.float32),
        in_specs=[anywhere] * 3 + [vmem] * 5,
        out_specs=vmem,
        scratch_shapes=[
            pltpu.VMEM((own_len, width), jnp.bfloat16),
            pltpu.VMEM(time.shape, jnp.bfloat16),
            pltpu.VMEM(channel.shape, jnp.bfloat16),
            pltpu.VMEM((width // LANES, SHARED, LANES), jnp.bfloat16),
            pltpu.VMEM((TAPS, width), jnp.bfloat16),
            pltpu.VMEM((2 * TAPS, width), jnp.float32),
            pltpu.VMEM((2 * BINS, width), jnp.float32),
            pltpu.VMEM((2 * BINS, width), jnp.float32),
            pltpu.VMEM((2 * BINS, LANES), jnp.float32),
            pltpu.VMEM((slabs, members, 2, bins, LANES), jnp.bfloat16),
            pltpu.VMEM((slabs, members, 2, bins, LANES), jnp.bfloat16),
            pltpu.VMEM((bins, 2 * SHARED, DMS), jnp.bfloat16),
            pltpu.VMEM((RADIX, SHARED, INNER), jnp.bfloat16),
            pltpu.VMEM((RADIX * bins, 2 * INNER), jnp.float32),
            pltpu.VMEM((members, kept, bins), jnp.float32),
            pltpu.VMEM((members, kept, bins), jnp.float32),
            dma((3,)), dma((1 + slabs,)), dma((1 + slabs,)),
            dma((slabs, members)), dma((slabs, members)), dma((members,)), dma((members,)),
        ],
        compiler_params=pltpu.CompilerParams(
            vmem_limit_bytes=56 * 2**20, collective_id=0, has_side_effects=True
        ),
    )(raw_samples, time, channel, filter_taps, units, dm_trials.reshape(1, DMS), tap, twiddle)
    return power[None]


def solution(mesh):
    in_specs = (P(("beam", "tm"), "freq"), P(None, "freq"), P(), P())
    out_specs = P(("beam", "tm"), "freq", None)
    return jax.shard_map(body, mesh=mesh, in_specs=in_specs, out_specs=out_specs, check_vma=False)
```

```python
import functools
import math

import jax
import jax.numpy as jnp
import numpy as np
from jax import lax
from jax.experimental import pallas as pl
from jax.experimental.pallas import tpu as pltpu
from jax.sharding import PartitionSpec as P

TAPS = 16
DFT_LEN = 2048
BINS = 256
SHARED = 512
DMS = 256
DM_STEPS = 1024
CHANNELS = 4096
RADIX = 8
INNER = CHANNELS // RADIX
CHUNK = 16
LANES = 128


def tables():
    bins = np.arange(BINS)[:, None]
    angle = 2 * np.pi * (bins * np.arange(DFT_LEN)[None, :] % DFT_LEN) / DFT_LEN
    time = np.concatenate([np.cos(angle), -np.sin(angle)], 0) / math.sqrt(DFT_LEN)
    angle = 2 * np.pi * (bins * np.arange(TAPS)[None, :]) / DFT_LEN
    tap = np.concatenate([np.cos(angle), -np.sin(angle)], 0)
    ids = np.arange(INNER)
    angle = 2 * np.pi * (np.arange(RADIX)[:, None] * ids[None, :]) / CHANNELS
    twiddle = np.stack([np.cos(angle), -np.sin(angle)]) / math.sqrt(RADIX)
    spread = ids.reshape(CHANNELS // LANES, LANES // RADIX).T.reshape(-1)
    angle = 2 * np.pi * (ids[:, None] * spread[None, :] % INNER) / INNER
    cosine, sine = np.cos(angle), np.sin(angle)
    channel = np.block([[cosine, -sine], [sine, cosine]]) / math.sqrt(INNER)
    return (
        jnp.asarray(time, jnp.bfloat16),
        jnp.asarray(tap, jnp.float32),
        jnp.asarray(twiddle, jnp.float32),
        jnp.asarray(channel, jnp.bfloat16),
    )


def unit_circle(phase):
    x = phase.astype(jnp.float32) * (2.0 * math.pi / DFT_LEN)
    y = x * x
    sine, cosine = jnp.full_like(y, -1 / 39916800), jnp.full_like(y, 1 / 479001600)
    for value in (1 / 362880, -1 / 5040, 1 / 120, -1 / 6, 1.0):
        sine = sine * y + value
    for value in (-1 / 3628800, 1 / 40320, -1 / 720, 1 / 24, -0.5, 1.0):
        cosine = cosine * y + value
    return cosine, sine * x


def fill_ramps(ramps, dms, first_bin, start, stop):
    bins = ramps.shape[0]

    @pl.loop(start, stop)
    def _(step):
        row = pl.multiple_of(step * CHUNK, CHUNK)
        units = lax.broadcasted_iota(jnp.int32, (CHUNK, DMS), 0) + (row + 1)
        delays = (units * dms[...]) >> 10
        turn_cos, turn_sin = unit_circle(delays)
        phase = (delays * first_bin) & (DFT_LEN - 1)
        quarter = phase >> 9
        cosine, sine = unit_circle(phase & 511)
        odd = (quarter & 1) == 1
        swapped_cos = jnp.where(odd, -sine, cosine)
        swapped_sin = jnp.where(odd, cosine, sine)
        far = quarter >= 2
        cosine = jnp.where(far, -swapped_cos, swapped_cos)
        sine = jnp.where(far, -swapped_sin, swapped_sin)
        for at in range(bins):
            ramps[at, pl.ds(row, CHUNK), :] = cosine.astype(jnp.bfloat16)
            ramps[at, pl.ds(SHARED + row, CHUNK), :] = sine.astype(jnp.bfloat16)
            if at + 1 < bins:
                cosine, sine = (
                    cosine * turn_cos - sine * turn_sin,
                    sine * turn_cos + cosine * turn_sin,
                )


def dft(real, imag):
    count = len(real)
    if count == 1:
        return real, imag
    er, ei = dft(real[0::2], imag[0::2])
    odr, odi = dft(real[1::2], imag[1::2])
    half = count // 2
    outs = [None] * count
    for k in range(half):
        if k == 0:
            tr, ti = odr[k], odi[k]
        elif 4 * k == count:
            tr, ti = odi[k], -odr[k]
        else:
            c, s = math.cos(2 * math.pi * k / count), math.sin(2 * math.pi * k / count)
            tr, ti = odr[k] * c + odi[k] * s, odi[k] * c - odr[k] * s
        outs[k] = (er[k] + tr, ei[k] + ti)
        outs[k + half] = (er[k] - tr, ei[k] - ti)
    return [o[0] for o in outs], [o[1] for o in outs]


def channelize(held, twiddle, first, slab):
    slabs, members, _, bins, _ = held.shape
    per = members // RADIX
    for src in range(per):
        lane = src * slabs + slab
        real, imag = [], []
        for n2 in range(RADIX):
            real.append(held[slab, n2 * per + src, 0].astype(jnp.float32))
            imag.append(held[slab, n2 * per + src, 1].astype(jnp.float32))
        real, imag = dft(real, imag)
        cols = slice(lane * 128, lane * 128 + 128)
        cols_imag = slice(INNER + lane * 128, INNER + lane * 128 + 128)
        for k2 in range(RADIX):
            c, s = twiddle[0, k2 : k2 + 1, cols], twiddle[1, k2 : k2 + 1, cols]
            rows = slice(k2 * bins, k2 * bins + bins)
            first[rows, cols] = real[k2] * c - imag[k2] * s
            first[rows, cols_imag] = real[k2] * s + imag[k2] * c


def fill_matches(matches, units):
    rows, lanes = units.shape
    ids = lax.broadcasted_iota(jnp.int32, (rows, SHARED), 1) + 1
    for k2 in range(RADIX):
        for at in range(lanes // RADIX):
            lane = at * RADIX + k2
            same = (units[:, lane : lane + 1] == ids).astype(jnp.float32)
            matches[k2, at * rows : (at + 1) * rows, :] = same.astype(jnp.bfloat16)


def group_units(spectra, matches, bins):
    grouped = jnp.zeros((2 * bins, SHARED), jnp.float32)
    whole = jnp.zeros((2 * bins, INNER), jnp.float32)
    for k2 in range(RADIX):
        part = spectra[k2 * bins : (k2 + 1) * bins]
        part = jnp.concatenate([part[:, :INNER], part[:, INNER:]], 0)
        part = part.astype(jnp.bfloat16)
        whole += part.astype(jnp.float32)
        grouped += jnp.dot(part, matches[k2], preferred_element_type=jnp.float32)
    rest = jnp.sum(whole, 1, keepdims=True) - jnp.sum(grouped, 1, keepdims=True)
    return grouped, rest


def partner_order(members):
    return sorted(range(1, members), key=lambda o: abs(o - members // 2))


def kernel(
    members, segments,
    raw, time_hbm, channel_hbm, filter_taps, units, dms, tap, twiddle,
    out,
    own, time, channel, later, tail, padded, spec, gain, extra, outgoing, held,
    ramps, matches, first, power_out, power_in,
    local_sem, halo_send, halo_recv, seg_send, seg_recv, pow_send, pow_recv,
):
    me = lax.axis_index("freq")
    seg = lax.axis_index("tm")
    own_len, width = own.shape
    bins = BINS // members
    kept = DMS // members
    loads = [
        pltpu.make_async_copy(raw, own, local_sem.at[0]),
        pltpu.make_async_copy(time_hbm, time, local_sem.at[1]),
        pltpu.make_async_copy(channel_hbm, channel, local_sem.at[2]),
    ]
    for load in loads[:2]:
        load.start()

    barrier = pltpu.get_barrier_semaphore()
    order = partner_order(members)
    for o in order:
        pl.semaphore_signal(
            barrier, inc=1, device_id={"freq": lax.rem(me + o, members)},
            device_id_type=pl.DeviceIdType.MESH,
        )

    @pl.when(seg > 0)
    def _():
        pl.semaphore_signal(
            barrier, inc=1, device_id={"tm": seg - 1}, device_id_type=pl.DeviceIdType.MESH
        )

    @pl.when(seg < segments - 1)
    def _():
        pl.semaphore_signal(
            barrier, inc=1, device_id={"tm": seg + 1}, device_id_type=pl.DeviceIdType.MESH
        )

    pl.semaphore_wait(
        barrier, members - 1 + jnp.minimum(seg, 1) + jnp.minimum(segments - 1 - seg, 1)
    )

    slabs = width // LANES

    def back_copy(slab):
        return pltpu.make_async_remote_copy(
            src_ref=raw.at[pl.ds(0, SHARED), pl.ds(slab * LANES, LANES)],
            dst_ref=later.at[slab],
            send_sem=halo_send.at[1 + slab], recv_sem=halo_recv.at[1 + slab],
            device_id={"tm": seg - 1}, device_id_type=pl.DeviceIdType.MESH,
        )

    def forward_copy():
        return pltpu.make_async_remote_copy(
            src_ref=raw.at[pl.ds(own_len - TAPS, TAPS)], dst_ref=tail,
            send_sem=halo_send.at[0], recv_sem=halo_recv.at[0],
            device_id={"tm": seg + 1}, device_id_type=pl.DeviceIdType.MESH,
        )

    @pl.when(seg > 0)
    def _():
        for slab in range(slabs):
            back_copy(slab).start()

    @pl.when(seg == 0)
    def _():
        tail[...] = jnp.zeros_like(tail)

    @pl.when(seg < segments - 1)
    def _():
        forward_copy().start()

    @pl.when(seg == segments - 1)
    def _():
        later[...] = jnp.zeros_like(later)

    loads[2].start()
    taps = filter_taps[...].astype(jnp.float32)
    padded[0:TAPS, :] = taps
    padded[TAPS:, :] = jnp.zeros_like(taps)
    gain[...] = jnp.dot(
        tap[...], taps, precision=lax.Precision.HIGHEST, preferred_element_type=jnp.float32
    )
    for load in loads[:2]:
        load.wait()
    spec[...] = jnp.dot(
        time[:, 0:own_len], own[...], preferred_element_type=jnp.float32
    )

    @pl.when(seg > 0)
    def _():
        forward_copy().wait_recv()

    def seg_copy(slab, slot, target):
        return pltpu.make_async_remote_copy(
            src_ref=outgoing.at[slab, target], dst_ref=held.at[slab, slot],
            send_sem=seg_send.at[slab, target], recv_sem=seg_recv.at[slab, slot],
            device_id={"freq": target}, device_id_type=pl.DeviceIdType.MESH,
        )

    def block(target, cols):
        row = pl.multiple_of(target * bins, bins)
        up, low = pl.ds(row, bins), pl.ds(BINS + row, bins)
        sr, si, gr, gi = spec[up, cols], spec[low, cols], gain[up, cols], gain[low, cols]
        real = sr * gr - si * gi + extra[up, :]
        imag = sr * gi + si * gr + extra[low, :]
        return real.astype(jnp.bfloat16), imag.astype(jnp.bfloat16)

    steps = SHARED // CHUNK // slabs
    for slab in range(slabs):
        cols = slice(slab * LANES, (slab + 1) * LANES)

        @pl.when(seg < segments - 1)
        def _():
            back_copy(slab).wait_recv()

        edge = tail[:, cols].astype(jnp.float32)
        edge = edge - later[slab, SHARED - TAPS :, :].astype(jnp.float32)
        fringe = jnp.zeros_like(edge)
        for e in range(1, TAPS):
            fringe = fringe + padded[e : e + TAPS, cols] * edge[TAPS - e : TAPS - e + 1]
        extra[...] = jnp.dot(
            tap[...], fringe * (1.0 / math.sqrt(DFT_LEN)),
            precision=lax.Precision.HIGHEST, preferred_element_type=jnp.float32,
        )
        spec[:, cols] += jnp.dot(
            time[:, own_len:], later[slab], preferred_element_type=jnp.float32
        )
        for o in order:
            target = lax.rem(me + o, members)
            outgoing[slab, target, 0], outgoing[slab, target, 1] = block(target, cols)
            seg_copy(slab, me, target).start()
        held[slab, me, 0], held[slab, me, 1] = block(me, cols)
        fill_ramps(ramps, dms, me * bins, slab * steps, (slab + 1) * steps)
    fill_matches(matches, units)

    for slab in range(slabs):
        for o in order:
            source = lax.rem(me + o, members)
            seg_copy(slab, source, source).wait_recv()
        channelize(held, twiddle, first, slab)
    loads[2].wait()
    spectra = jnp.dot(
        first[...].astype(jnp.bfloat16), channel[...], preferred_element_type=jnp.float32
    )
    grouped, rest = group_units(spectra, matches, bins)
    real, imag = grouped[:bins], grouped[bins:]
    upper = jnp.concatenate([real, -imag], 1)
    lower = jnp.concatenate([imag, real], 1)
    rows = []
    for at in range(bins):
        left = jnp.concatenate([upper[at : at + 1], lower[at : at + 1]], 0)
        total = jnp.dot(
            left.astype(jnp.bfloat16), ramps[at], preferred_element_type=jnp.float32
        )
        re = total[0:1] + rest[at : at + 1]
        im = total[1:2] + rest[bins + at : bins + at + 1]
        rows.append((re * re + im * im) * (1.0 / CHANNELS))
    turned = jnp.concatenate(rows, 0).T
    for target in range(members):
        power_out[target] = turned[target * kept : (target + 1) * kept]

    def power_copy(slot, target):
        return pltpu.make_async_remote_copy(
            src_ref=power_out.at[target], dst_ref=power_in.at[slot],
            send_sem=pow_send.at[target], recv_sem=pow_recv.at[slot],
            device_id={"freq": target}, device_id_type=pl.DeviceIdType.MESH,
        )

    for o in order:
        power_copy(me, lax.rem(me + o, members)).start()
    power_in[me] = power_out[me]
    for o in order:
        target = lax.rem(me + o, members)
        power_copy(target, target).wait_recv()
    out[...] = jnp.concatenate([power_in[source] for source in range(members)], 1)
    for o in order:
        target = lax.rem(me + o, members)
        for slab in range(slabs):
            seg_copy(slab, target, target).wait_send()
        power_copy(target, target).wait_send()

    @pl.when(seg > 0)
    def _():
        for slab in range(slabs):
            back_copy(slab).wait_send()

    @pl.when(seg < segments - 1)
    def _():
        forward_copy().wait_send()


def body(raw_samples, filter_taps, dm_trials, channel_units):
    members = lax.axis_size("freq")
    own_len, width = raw_samples.shape
    bins, kept, slabs = BINS // members, DMS // members, width // LANES
    time, tap, twiddle, channel = tables()
    units = channel_units.reshape(CHANNELS // LANES, LANES)
    vmem = pl.BlockSpec(memory_space=pltpu.VMEM)
    anywhere = pl.BlockSpec(memory_space=pl.ANY)
    dma = pltpu.SemaphoreType.DMA
    power = pl.pallas_call(
        functools.partial(kernel, members, lax.axis_size("tm")),
        out_shape=jax.ShapeDtypeStruct((kept, BINS), jnp.float32),
        in_specs=[anywhere] * 3 + [vmem] * 5,
        out_specs=vmem,
        scratch_shapes=[
            pltpu.VMEM((own_len, width), jnp.bfloat16),
            pltpu.VMEM(time.shape, jnp.bfloat16),
            pltpu.VMEM(channel.shape, jnp.bfloat16),
            pltpu.VMEM((width // LANES, SHARED, LANES), jnp.bfloat16),
            pltpu.VMEM((TAPS, width), jnp.bfloat16),
            pltpu.VMEM((2 * TAPS, width), jnp.float32),
            pltpu.VMEM((2 * BINS, width), jnp.float32),
            pltpu.VMEM((2 * BINS, width), jnp.float32),
            pltpu.VMEM((2 * BINS, LANES), jnp.float32),
            pltpu.VMEM((slabs, members, 2, bins, LANES), jnp.bfloat16),
            pltpu.VMEM((slabs, members, 2, bins, LANES), jnp.bfloat16),
            pltpu.VMEM((bins, 2 * SHARED, DMS), jnp.bfloat16),
            pltpu.VMEM((RADIX, INNER, SHARED), jnp.bfloat16),
            pltpu.VMEM((RADIX * bins, 2 * INNER), jnp.float32),
            pltpu.VMEM((members, kept, bins), jnp.float32),
            pltpu.VMEM((members, kept, bins), jnp.float32),
            dma((3,)), dma((1 + slabs,)), dma((1 + slabs,)),
            dma((slabs, members)), dma((slabs, members)), dma((members,)), dma((members,)),
        ],
        compiler_params=pltpu.CompilerParams(
            vmem_limit_bytes=56 * 2**20, collective_id=0, has_side_effects=True
        ),
    )(raw_samples, time, channel, filter_taps, units, dm_trials.reshape(1, DMS), tap, twiddle)
    return power[None]


def solution(mesh):
    in_specs = (P(("beam", "tm"), "freq"), P(None, "freq"), P(), P())
    out_specs = P(("beam", "tm"), "freq", None)
    return jax.shard_map(body, mesh=mesh, in_specs=in_specs, out_specs=out_specs, check_vma=False)
```

```python
import functools
import math

import jax
import jax.numpy as jnp
import numpy as np
from jax import lax
from jax.experimental import pallas as pl
from jax.experimental.pallas import tpu as pltpu
from jax.sharding import PartitionSpec as P

TAPS = 16
DFT_LEN = 2048
BINS = 256
SHARED = 512
DMS = 256
DM_STEPS = 1024
CHANNELS = 4096
RADIX = 8
INNER = CHANNELS // RADIX
CHUNK = 16
LANES = 128


def tables():
    bins = np.arange(BINS)[:, None]
    angle = 2 * np.pi * (bins * np.arange(DFT_LEN)[None, :] % DFT_LEN) / DFT_LEN
    time = np.concatenate([np.cos(angle), -np.sin(angle)], 0) / math.sqrt(DFT_LEN)
    angle = 2 * np.pi * (bins * np.arange(TAPS)[None, :]) / DFT_LEN
    tap = np.concatenate([np.cos(angle), -np.sin(angle)], 0)
    ids = np.arange(INNER)
    angle = 2 * np.pi * (np.arange(RADIX)[:, None] * ids[None, :]) / CHANNELS
    twiddle = np.stack([np.cos(angle), -np.sin(angle)]) / math.sqrt(RADIX)
    spread = ids.reshape(CHANNELS // LANES, LANES // RADIX).T.reshape(-1)
    angle = 2 * np.pi * (ids[:, None] * spread[None, :] % INNER) / INNER
    cosine, sine = np.cos(angle), np.sin(angle)
    channel = np.block([[cosine, -sine], [sine, cosine]]) / math.sqrt(INNER)
    return (
        jnp.asarray(time, jnp.bfloat16),
        jnp.asarray(tap, jnp.float32),
        jnp.asarray(twiddle, jnp.float32),
        jnp.asarray(channel, jnp.bfloat16),
    )


def unit_circle(phase):
    x = phase.astype(jnp.float32) * (2.0 * math.pi / DFT_LEN)
    y = x * x
    sine, cosine = jnp.full_like(y, -1 / 39916800), jnp.full_like(y, 1 / 479001600)
    for value in (1 / 362880, -1 / 5040, 1 / 120, -1 / 6, 1.0):
        sine = sine * y + value
    for value in (-1 / 3628800, 1 / 40320, -1 / 720, 1 / 24, -0.5, 1.0):
        cosine = cosine * y + value
    return cosine, sine * x


def fill_ramps(ramps, dms, first_bin, start, stop):
    bins = ramps.shape[0]

    @pl.loop(start, stop)
    def _(step):
        row = pl.multiple_of(step * CHUNK, CHUNK)
        units = lax.broadcasted_iota(jnp.int32, (CHUNK, DMS), 0) + (row + 1)
        delays = (units * dms[...]) >> 10
        turn_cos, turn_sin = unit_circle(delays)
        phase = (delays * first_bin) & (DFT_LEN - 1)
        quarter = phase >> 9
        cosine, sine = unit_circle(phase & 511)
        odd = (quarter & 1) == 1
        swapped_cos = jnp.where(odd, -sine, cosine)
        swapped_sin = jnp.where(odd, cosine, sine)
        far = quarter >= 2
        cosine = jnp.where(far, -swapped_cos, swapped_cos)
        sine = jnp.where(far, -swapped_sin, swapped_sin)
        for at in range(bins):
            ramps[at, pl.ds(row, CHUNK), :] = cosine.astype(jnp.bfloat16)
            ramps[at, pl.ds(SHARED + row, CHUNK), :] = sine.astype(jnp.bfloat16)
            if at + 1 < bins:
                cosine, sine = (
                    cosine * turn_cos - sine * turn_sin,
                    sine * turn_cos + cosine * turn_sin,
                )


def dft(real, imag):
    count = len(real)
    if count == 1:
        return real, imag
    er, ei = dft(real[0::2], imag[0::2])
    odr, odi = dft(real[1::2], imag[1::2])
    half = count // 2
    outs = [None] * count
    for k in range(half):
        if k == 0:
            tr, ti = odr[k], odi[k]
        elif 4 * k == count:
            tr, ti = odi[k], -odr[k]
        else:
            c, s = math.cos(2 * math.pi * k / count), math.sin(2 * math.pi * k / count)
            tr, ti = odr[k] * c + odi[k] * s, odi[k] * c - odr[k] * s
        outs[k] = (er[k] + tr, ei[k] + ti)
        outs[k + half] = (er[k] - tr, ei[k] - ti)
    return [o[0] for o in outs], [o[1] for o in outs]


def channelize(held, twiddle, first, slab):
    slabs, members, _, bins, _ = held.shape
    per = members // RADIX
    for src in range(per):
        lane = src * slabs + slab
        real, imag = [], []
        for n2 in range(RADIX):
            real.append(held[slab, n2 * per + src, 0].astype(jnp.float32))
            imag.append(held[slab, n2 * per + src, 1].astype(jnp.float32))
        real, imag = dft(real, imag)
        cols = slice(lane * 128, lane * 128 + 128)
        cols_imag = slice(INNER + lane * 128, INNER + lane * 128 + 128)
        for k2 in range(RADIX):
            c, s = twiddle[0, k2 : k2 + 1, cols], twiddle[1, k2 : k2 + 1, cols]
            rows = slice(k2 * bins, k2 * bins + bins)
            first[rows, cols] = real[k2] * c - imag[k2] * s
            first[rows, cols_imag] = real[k2] * s + imag[k2] * c


def fill_matches(matches, units):
    rows, lanes = units.shape
    ids = lax.broadcasted_iota(jnp.int32, (rows, SHARED), 1) + 1
    for k2 in range(RADIX):
        for at in range(lanes // RADIX):
            lane = at * RADIX + k2
            same = (units[:, lane : lane + 1] == ids).astype(jnp.float32)
            matches[k2, at * rows : (at + 1) * rows, :] = same.astype(jnp.bfloat16)


def group_units(spectra, matches, bins):
    grouped = jnp.zeros((2 * bins, SHARED), jnp.float32)
    whole = jnp.zeros((2 * bins, INNER), jnp.float32)
    for k2 in range(RADIX):
        part = spectra[k2 * bins : (k2 + 1) * bins]
        part = jnp.concatenate([part[:, :INNER], part[:, INNER:]], 0)
        part = part.astype(jnp.bfloat16)
        whole += part.astype(jnp.float32)
        grouped += jnp.dot(part, matches[k2], preferred_element_type=jnp.float32)
    rest = jnp.sum(whole, 1, keepdims=True) - jnp.sum(grouped, 1, keepdims=True)
    return grouped, rest


def partner_order(members):
    return sorted(range(1, members), key=lambda o: abs(o - members // 2))


def kernel(
    members, segments,
    raw, time_hbm, channel_hbm, filter_taps, units, dms, tap, twiddle,
    out,
    own, time, channel, later, tail, padded, spec, gain, extra, outgoing, held,
    ramps, matches, first, power_out, power_in,
    local_sem, halo_send, halo_recv, seg_send, seg_recv, pow_send, pow_recv,
):
    me = lax.axis_index("freq")
    seg = lax.axis_index("tm")
    own_len, width = own.shape
    bins = BINS // members
    kept = DMS // members
    loads = [
        pltpu.make_async_copy(raw, own, local_sem.at[0]),
        pltpu.make_async_copy(time_hbm, time, local_sem.at[1]),
        pltpu.make_async_copy(channel_hbm, channel, local_sem.at[2]),
    ]
    for load in loads[:2]:
        load.start()

    barrier = pltpu.get_barrier_semaphore()
    order = partner_order(members)
    for o in order:
        pl.semaphore_signal(
            barrier, inc=1, device_id={"freq": lax.rem(me + o, members)},
            device_id_type=pl.DeviceIdType.MESH,
        )

    @pl.when(seg > 0)
    def _():
        pl.semaphore_signal(
            barrier, inc=1, device_id={"tm": seg - 1}, device_id_type=pl.DeviceIdType.MESH
        )

    @pl.when(seg < segments - 1)
    def _():
        pl.semaphore_signal(
            barrier, inc=1, device_id={"tm": seg + 1}, device_id_type=pl.DeviceIdType.MESH
        )

    pl.semaphore_wait(
        barrier, members - 1 + jnp.minimum(seg, 1) + jnp.minimum(segments - 1 - seg, 1)
    )

    slabs = width // LANES

    def back_copy(slab):
        return pltpu.make_async_remote_copy(
            src_ref=raw.at[pl.ds(0, SHARED), pl.ds(slab * LANES, LANES)],
            dst_ref=later.at[slab],
            send_sem=halo_send.at[1 + slab], recv_sem=halo_recv.at[1 + slab],
            device_id={"tm": seg - 1}, device_id_type=pl.DeviceIdType.MESH,
        )

    def forward_copy():
        return pltpu.make_async_remote_copy(
            src_ref=raw.at[pl.ds(own_len - TAPS, TAPS)], dst_ref=tail,
            send_sem=halo_send.at[0], recv_sem=halo_recv.at[0],
            device_id={"tm": seg + 1}, device_id_type=pl.DeviceIdType.MESH,
        )

    @pl.when(seg > 0)
    def _():
        for slab in range(slabs):
            back_copy(slab).start()

    @pl.when(seg == 0)
    def _():
        tail[...] = jnp.zeros_like(tail)

    @pl.when(seg < segments - 1)
    def _():
        forward_copy().start()

    @pl.when(seg == segments - 1)
    def _():
        later[...] = jnp.zeros_like(later)

    loads[2].start()
    taps = filter_taps[...].astype(jnp.float32)
    padded[0:TAPS, :] = taps
    padded[TAPS:, :] = jnp.zeros_like(taps)
    gain[...] = jnp.dot(
        tap[...], taps, precision=lax.Precision.HIGHEST, preferred_element_type=jnp.float32
    )
    for load in loads[:2]:
        load.wait()
    spec[...] = jnp.dot(
        time[:, 0:own_len], own[...], preferred_element_type=jnp.float32
    )

    @pl.when(seg > 0)
    def _():
        forward_copy().wait_recv()

    def seg_copy(slab, slot, target):
        return pltpu.make_async_remote_copy(
            src_ref=outgoing.at[slab, target], dst_ref=held.at[slab, slot],
            send_sem=seg_send.at[slab, target], recv_sem=seg_recv.at[slab, slot],
            device_id={"freq": target}, device_id_type=pl.DeviceIdType.MESH,
        )

    def block(target, cols):
        row = pl.multiple_of(target * bins, bins)
        up, low = pl.ds(row, bins), pl.ds(BINS + row, bins)
        sr, si, gr, gi = spec[up, cols], spec[low, cols], gain[up, cols], gain[low, cols]
        real = sr * gr - si * gi + extra[up, :]
        imag = sr * gi + si * gr + extra[low, :]
        return real.astype(jnp.bfloat16), imag.astype(jnp.bfloat16)

    early = SHARED // CHUNK // 2
    steps = early // slabs
    fill_ramps(ramps, dms, me * bins, 0, early)
    for slab in range(slabs):
        cols = slice(slab * LANES, (slab + 1) * LANES)

        @pl.when(seg < segments - 1)
        def _():
            back_copy(slab).wait_recv()

        edge = tail[:, cols].astype(jnp.float32)
        edge = edge - later[slab, SHARED - TAPS :, :].astype(jnp.float32)
        fringe = jnp.zeros_like(edge)
        for e in range(1, TAPS):
            fringe = fringe + padded[e : e + TAPS, cols] * edge[TAPS - e : TAPS - e + 1]
        extra[...] = jnp.dot(
            tap[...], fringe * (1.0 / math.sqrt(DFT_LEN)),
            precision=lax.Precision.HIGHEST, preferred_element_type=jnp.float32,
        )
        spec[:, cols] += jnp.dot(
            time[:, own_len:], later[slab], preferred_element_type=jnp.float32
        )
        for o in order:
            target = lax.rem(me + o, members)
            outgoing[slab, target, 0], outgoing[slab, target, 1] = block(target, cols)
            seg_copy(slab, me, target).start()
        held[slab, me, 0], held[slab, me, 1] = block(me, cols)
        fill_ramps(
            ramps, dms, me * bins, early + slab * steps, early + (slab + 1) * steps
        )
    fill_matches(matches, units)

    for slab in range(slabs):
        for o in order:
            source = lax.rem(me + o, members)
            seg_copy(slab, source, source).wait_recv()
        channelize(held, twiddle, first, slab)
    loads[2].wait()
    spectra = jnp.dot(
        first[...].astype(jnp.bfloat16), channel[...], preferred_element_type=jnp.float32
    )
    grouped, rest = group_units(spectra, matches, bins)
    real, imag = grouped[:bins], grouped[bins:]
    upper = jnp.concatenate([real, -imag], 1)
    lower = jnp.concatenate([imag, real], 1)
    rows = []
    for at in range(bins):
        left = jnp.concatenate([upper[at : at + 1], lower[at : at + 1]], 0)
        total = jnp.dot(
            left.astype(jnp.bfloat16), ramps[at], preferred_element_type=jnp.float32
        )
        re = total[0:1] + rest[at : at + 1]
        im = total[1:2] + rest[bins + at : bins + at + 1]
        rows.append((re * re + im * im) * (1.0 / CHANNELS))
    turned = jnp.concatenate(rows, 0).T
    for target in range(members):
        power_out[target] = turned[target * kept : (target + 1) * kept]

    def power_copy(slot, target):
        return pltpu.make_async_remote_copy(
            src_ref=power_out.at[target], dst_ref=power_in.at[slot],
            send_sem=pow_send.at[target], recv_sem=pow_recv.at[slot],
            device_id={"freq": target}, device_id_type=pl.DeviceIdType.MESH,
        )

    for o in order:
        power_copy(me, lax.rem(me + o, members)).start()
    power_in[me] = power_out[me]
    for o in order:
        target = lax.rem(me + o, members)
        power_copy(target, target).wait_recv()
    out[...] = jnp.concatenate([power_in[source] for source in range(members)], 1)
    for o in order:
        target = lax.rem(me + o, members)
        for slab in range(slabs):
            seg_copy(slab, target, target).wait_send()
        power_copy(target, target).wait_send()

    @pl.when(seg > 0)
    def _():
        for slab in range(slabs):
            back_copy(slab).wait_send()

    @pl.when(seg < segments - 1)
    def _():
        forward_copy().wait_send()


def body(raw_samples, filter_taps, dm_trials, channel_units):
    members = lax.axis_size("freq")
    own_len, width = raw_samples.shape
    bins, kept, slabs = BINS // members, DMS // members, width // LANES
    time, tap, twiddle, channel = tables()
    units = channel_units.reshape(CHANNELS // LANES, LANES)
    vmem = pl.BlockSpec(memory_space=pltpu.VMEM)
    anywhere = pl.BlockSpec(memory_space=pl.ANY)
    dma = pltpu.SemaphoreType.DMA
    power = pl.pallas_call(
        functools.partial(kernel, members, lax.axis_size("tm")),
        out_shape=jax.ShapeDtypeStruct((kept, BINS), jnp.float32),
        in_specs=[anywhere] * 3 + [vmem] * 5,
        out_specs=vmem,
        scratch_shapes=[
            pltpu.VMEM((own_len, width), jnp.bfloat16),
            pltpu.VMEM(time.shape, jnp.bfloat16),
            pltpu.VMEM(channel.shape, jnp.bfloat16),
            pltpu.VMEM((width // LANES, SHARED, LANES), jnp.bfloat16),
            pltpu.VMEM((TAPS, width), jnp.bfloat16),
            pltpu.VMEM((2 * TAPS, width), jnp.float32),
            pltpu.VMEM((2 * BINS, width), jnp.float32),
            pltpu.VMEM((2 * BINS, width), jnp.float32),
            pltpu.VMEM((2 * BINS, LANES), jnp.float32),
            pltpu.VMEM((slabs, members, 2, bins, LANES), jnp.bfloat16),
            pltpu.VMEM((slabs, members, 2, bins, LANES), jnp.bfloat16),
            pltpu.VMEM((bins, 2 * SHARED, DMS), jnp.bfloat16),
            pltpu.VMEM((RADIX, INNER, SHARED), jnp.bfloat16),
            pltpu.VMEM((RADIX * bins, 2 * INNER), jnp.float32),
            pltpu.VMEM((members, kept, bins), jnp.float32),
            pltpu.VMEM((members, kept, bins), jnp.float32),
            dma((3,)), dma((1 + slabs,)), dma((1 + slabs,)),
            dma((slabs, members)), dma((slabs, members)), dma((members,)), dma((members,)),
        ],
        compiler_params=pltpu.CompilerParams(
            vmem_limit_bytes=56 * 2**20, collective_id=0, has_side_effects=True
        ),
    )(raw_samples, time, channel, filter_taps, units, dm_trials.reshape(1, DMS), tap, twiddle)
    return power[None]


def solution(mesh):
    in_specs = (P(("beam", "tm"), "freq"), P(None, "freq"), P(), P())
    out_specs = P(("beam", "tm"), "freq", None)
    return jax.shard_map(body, mesh=mesh, in_specs=in_specs, out_specs=out_specs, check_vma=False)
```

```python
import functools
import math

import jax
import jax.numpy as jnp
import numpy as np
from jax import lax
from jax.experimental import pallas as pl
from jax.experimental.pallas import tpu as pltpu
from jax.sharding import PartitionSpec as P

TAPS = 16
DFT_LEN = 2048
BINS = 256
SHARED = 512
DMS = 256
DM_STEPS = 1024
CHANNELS = 4096
RADIX = 8
INNER = CHANNELS // RADIX
CHUNK = 16
LANES = 128


def tables():
    bins = np.arange(BINS)[:, None]
    angle = 2 * np.pi * (bins * np.arange(DFT_LEN)[None, :] % DFT_LEN) / DFT_LEN
    time = np.concatenate([np.cos(angle), -np.sin(angle)], 0) / math.sqrt(DFT_LEN)
    angle = 2 * np.pi * (bins * np.arange(TAPS)[None, :]) / DFT_LEN
    tap = np.concatenate([np.cos(angle), -np.sin(angle)], 0)
    ids = np.arange(INNER)
    angle = 2 * np.pi * (np.arange(RADIX)[:, None] * ids[None, :]) / CHANNELS
    twiddle = np.stack([np.cos(angle), -np.sin(angle)]) / math.sqrt(RADIX)
    spread = ids.reshape(CHANNELS // LANES, LANES // RADIX).T.reshape(-1)
    angle = 2 * np.pi * (ids[:, None] * spread[None, :] % INNER) / INNER
    cosine, sine = np.cos(angle), np.sin(angle)
    channel = np.block([[cosine, -sine], [sine, cosine]]) / math.sqrt(INNER)
    return (
        jnp.asarray(time, jnp.bfloat16),
        jnp.asarray(tap, jnp.float32),
        jnp.asarray(twiddle, jnp.float32),
        jnp.asarray(channel, jnp.bfloat16),
    )


def unit_circle(phase):
    x = phase.astype(jnp.float32) * (2.0 * math.pi / DFT_LEN)
    y = x * x
    sine, cosine = jnp.full_like(y, -1 / 39916800), jnp.full_like(y, 1 / 479001600)
    for value in (1 / 362880, -1 / 5040, 1 / 120, -1 / 6, 1.0):
        sine = sine * y + value
    for value in (-1 / 3628800, 1 / 40320, -1 / 720, 1 / 24, -0.5, 1.0):
        cosine = cosine * y + value
    return cosine, sine * x


def fill_ramps(ramps, dms, first_bin, start, stop):
    bins = ramps.shape[0]

    @pl.loop(start, stop)
    def _(step):
        row = pl.multiple_of(step * CHUNK, CHUNK)
        units = lax.broadcasted_iota(jnp.int32, (CHUNK, DMS), 0) + (row + 1)
        delays = (units * dms[...]) >> 10
        turn_cos, turn_sin = unit_circle(delays)
        phase = (delays * first_bin) & (DFT_LEN - 1)
        quarter = phase >> 9
        cosine, sine = unit_circle(phase & 511)
        odd = (quarter & 1) == 1
        swapped_cos = jnp.where(odd, -sine, cosine)
        swapped_sin = jnp.where(odd, cosine, sine)
        far = quarter >= 2
        cosine = jnp.where(far, -swapped_cos, swapped_cos)
        sine = jnp.where(far, -swapped_sin, swapped_sin)
        for at in range(bins):
            ramps[at, pl.ds(row, CHUNK), :] = cosine.astype(jnp.bfloat16)
            ramps[at, pl.ds(SHARED + row, CHUNK), :] = sine.astype(jnp.bfloat16)
            if at + 1 < bins:
                cosine, sine = (
                    cosine * turn_cos - sine * turn_sin,
                    sine * turn_cos + cosine * turn_sin,
                )


def dft(real, imag):
    count = len(real)
    if count == 1:
        return real, imag
    er, ei = dft(real[0::2], imag[0::2])
    odr, odi = dft(real[1::2], imag[1::2])
    half = count // 2
    outs = [None] * count
    for k in range(half):
        if k == 0:
            tr, ti = odr[k], odi[k]
        elif 4 * k == count:
            tr, ti = odi[k], -odr[k]
        else:
            c, s = math.cos(2 * math.pi * k / count), math.sin(2 * math.pi * k / count)
            tr, ti = odr[k] * c + odi[k] * s, odi[k] * c - odr[k] * s
        outs[k] = (er[k] + tr, ei[k] + ti)
        outs[k + half] = (er[k] - tr, ei[k] - ti)
    return [o[0] for o in outs], [o[1] for o in outs]


def channelize(held, twiddle, first, slab):
    slabs, members, _, bins, _ = held.shape
    per = members // RADIX
    for src in range(per):
        lane = src * slabs + slab
        real, imag = [], []
        for n2 in range(RADIX):
            real.append(held[slab, n2 * per + src, 0].astype(jnp.float32))
            imag.append(held[slab, n2 * per + src, 1].astype(jnp.float32))
        real, imag = dft(real, imag)
        cols = slice(lane * 128, lane * 128 + 128)
        cols_imag = slice(INNER + lane * 128, INNER + lane * 128 + 128)
        for k2 in range(RADIX):
            c, s = twiddle[0, k2 : k2 + 1, cols], twiddle[1, k2 : k2 + 1, cols]
            rows = slice(k2 * bins, k2 * bins + bins)
            first[rows, cols] = real[k2] * c - imag[k2] * s
            first[rows, cols_imag] = real[k2] * s + imag[k2] * c


def fill_matches(matches, units):
    rows, lanes = units.shape
    ids = lax.broadcasted_iota(jnp.int32, (rows, SHARED), 1) + 1
    for k2 in range(RADIX):
        for at in range(lanes // RADIX):
            lane = at * RADIX + k2
            same = (units[:, lane : lane + 1] == ids).astype(jnp.float32)
            matches[k2, at * rows : (at + 1) * rows, :] = same.astype(jnp.bfloat16)


def group_units(spectra, matches, bins):
    grouped = jnp.zeros((2 * bins, SHARED), jnp.float32)
    whole = jnp.zeros((2 * bins, INNER), jnp.float32)
    for k2 in range(RADIX):
        part = spectra[k2 * bins : (k2 + 1) * bins]
        part = jnp.concatenate([part[:, :INNER], part[:, INNER:]], 0)
        part = part.astype(jnp.bfloat16)
        whole += part.astype(jnp.float32)
        grouped += jnp.dot(part, matches[k2], preferred_element_type=jnp.float32)
    rest = jnp.sum(whole, 1, keepdims=True) - jnp.sum(grouped, 1, keepdims=True)
    return grouped, rest


def partner_order(members):
    return sorted(range(1, members), key=lambda o: -abs(o - members // 2))


def kernel(
    members, segments,
    raw, time_hbm, channel_hbm, filter_taps, units, dms, tap, twiddle,
    out,
    own, time, channel, later, tail, padded, spec, gain, extra, outgoing, held,
    ramps, matches, first, power_out, power_in,
    local_sem, halo_send, halo_recv, seg_send, seg_recv, pow_send, pow_recv,
):
    me = lax.axis_index("freq")
    seg = lax.axis_index("tm")
    own_len, width = own.shape
    bins = BINS // members
    kept = DMS // members
    loads = [
        pltpu.make_async_copy(raw, own, local_sem.at[0]),
        pltpu.make_async_copy(time_hbm, time, local_sem.at[1]),
        pltpu.make_async_copy(channel_hbm, channel, local_sem.at[2]),
    ]
    for load in loads[:2]:
        load.start()

    barrier = pltpu.get_barrier_semaphore()
    order = partner_order(members)
    for o in order:
        pl.semaphore_signal(
            barrier, inc=1, device_id={"freq": lax.rem(me + o, members)},
            device_id_type=pl.DeviceIdType.MESH,
        )

    @pl.when(seg > 0)
    def _():
        pl.semaphore_signal(
            barrier, inc=1, device_id={"tm": seg - 1}, device_id_type=pl.DeviceIdType.MESH
        )

    @pl.when(seg < segments - 1)
    def _():
        pl.semaphore_signal(
            barrier, inc=1, device_id={"tm": seg + 1}, device_id_type=pl.DeviceIdType.MESH
        )

    pl.semaphore_wait(
        barrier, members - 1 + jnp.minimum(seg, 1) + jnp.minimum(segments - 1 - seg, 1)
    )

    slabs = width // LANES

    def back_copy(slab):
        return pltpu.make_async_remote_copy(
            src_ref=raw.at[pl.ds(0, SHARED), pl.ds(slab * LANES, LANES)],
            dst_ref=later.at[slab],
            send_sem=halo_send.at[1 + slab], recv_sem=halo_recv.at[1 + slab],
            device_id={"tm": seg - 1}, device_id_type=pl.DeviceIdType.MESH,
        )

    def forward_copy():
        return pltpu.make_async_remote_copy(
            src_ref=raw.at[pl.ds(own_len - TAPS, TAPS)], dst_ref=tail,
            send_sem=halo_send.at[0], recv_sem=halo_recv.at[0],
            device_id={"tm": seg + 1}, device_id_type=pl.DeviceIdType.MESH,
        )

    @pl.when(seg > 0)
    def _():
        for slab in range(slabs):
            back_copy(slab).start()

    @pl.when(seg == 0)
    def _():
        tail[...] = jnp.zeros_like(tail)

    @pl.when(seg < segments - 1)
    def _():
        forward_copy().start()

    @pl.when(seg == segments - 1)
    def _():
        later[...] = jnp.zeros_like(later)

    loads[2].start()
    taps = filter_taps[...].astype(jnp.float32)
    padded[0:TAPS, :] = taps
    padded[TAPS:, :] = jnp.zeros_like(taps)
    gain[...] = jnp.dot(
        tap[...], taps, precision=lax.Precision.HIGHEST, preferred_element_type=jnp.float32
    )
    for load in loads[:2]:
        load.wait()
    spec[...] = jnp.dot(
        time[:, 0:own_len], own[...], preferred_element_type=jnp.float32
    )

    @pl.when(seg > 0)
    def _():
        forward_copy().wait_recv()

    def seg_copy(slab, slot, target):
        return pltpu.make_async_remote_copy(
            src_ref=outgoing.at[slab, target], dst_ref=held.at[slab, slot],
            send_sem=seg_send.at[slab, target], recv_sem=seg_recv.at[slab, slot],
            device_id={"freq": target}, device_id_type=pl.DeviceIdType.MESH,
        )

    def block(target, cols):
        row = pl.multiple_of(target * bins, bins)
        up, low = pl.ds(row, bins), pl.ds(BINS + row, bins)
        sr, si, gr, gi = spec[up, cols], spec[low, cols], gain[up, cols], gain[low, cols]
        real = sr * gr - si * gi + extra[up, :]
        imag = sr * gi + si * gr + extra[low, :]
        return real.astype(jnp.bfloat16), imag.astype(jnp.bfloat16)

    steps = SHARED // CHUNK // slabs
    for slab in range(slabs):
        cols = slice(slab * LANES, (slab + 1) * LANES)

        @pl.when(seg < segments - 1)
        def _():
            back_copy(slab).wait_recv()

        edge = tail[:, cols].astype(jnp.float32)
        edge = edge - later[slab, SHARED - TAPS :, :].astype(jnp.float32)
        fringe = jnp.zeros_like(edge)
        for e in range(1, TAPS):
            fringe = fringe + padded[e : e + TAPS, cols] * edge[TAPS - e : TAPS - e + 1]
        extra[...] = jnp.dot(
            tap[...], fringe * (1.0 / math.sqrt(DFT_LEN)),
            precision=lax.Precision.HIGHEST, preferred_element_type=jnp.float32,
        )
        spec[:, cols] += jnp.dot(
            time[:, own_len:], later[slab], preferred_element_type=jnp.float32
        )
        for o in order:
            target = lax.rem(me + o, members)
            outgoing[slab, target, 0], outgoing[slab, target, 1] = block(target, cols)
            seg_copy(slab, me, target).start()
        held[slab, me, 0], held[slab, me, 1] = block(me, cols)
        fill_ramps(ramps, dms, me * bins, slab * steps, (slab + 1) * steps)
    fill_matches(matches, units)

    for slab in range(slabs):
        for o in order:
            source = lax.rem(me + o, members)
            seg_copy(slab, source, source).wait_recv()
        channelize(held, twiddle, first, slab)
    loads[2].wait()
    spectra = jnp.dot(
        first[...].astype(jnp.bfloat16), channel[...], preferred_element_type=jnp.float32
    )
    grouped, rest = group_units(spectra, matches, bins)
    real, imag = grouped[:bins], grouped[bins:]
    upper = jnp.concatenate([real, -imag], 1)
    lower = jnp.concatenate([imag, real], 1)
    rows = []
    for at in range(bins):
        left = jnp.concatenate([upper[at : at + 1], lower[at : at + 1]], 0)
        total = jnp.dot(
            left.astype(jnp.bfloat16), ramps[at], preferred_element_type=jnp.float32
        )
        re = total[0:1] + rest[at : at + 1]
        im = total[1:2] + rest[bins + at : bins + at + 1]
        rows.append((re * re + im * im) * (1.0 / CHANNELS))
    turned = jnp.concatenate(rows, 0).T
    for target in range(members):
        power_out[target] = turned[target * kept : (target + 1) * kept]

    def power_copy(slot, target):
        return pltpu.make_async_remote_copy(
            src_ref=power_out.at[target], dst_ref=power_in.at[slot],
            send_sem=pow_send.at[target], recv_sem=pow_recv.at[slot],
            device_id={"freq": target}, device_id_type=pl.DeviceIdType.MESH,
        )

    for o in order:
        power_copy(me, lax.rem(me + o, members)).start()
    power_in[me] = power_out[me]
    for o in order:
        target = lax.rem(me + o, members)
        power_copy(target, target).wait_recv()
    out[...] = jnp.concatenate([power_in[source] for source in range(members)], 1)
    for o in order:
        target = lax.rem(me + o, members)
        for slab in range(slabs):
            seg_copy(slab, target, target).wait_send()
        power_copy(target, target).wait_send()

    @pl.when(seg > 0)
    def _():
        for slab in range(slabs):
            back_copy(slab).wait_send()

    @pl.when(seg < segments - 1)
    def _():
        forward_copy().wait_send()


def body(raw_samples, filter_taps, dm_trials, channel_units):
    members = lax.axis_size("freq")
    own_len, width = raw_samples.shape
    bins, kept, slabs = BINS // members, DMS // members, width // LANES
    time, tap, twiddle, channel = tables()
    units = channel_units.reshape(CHANNELS // LANES, LANES)
    vmem = pl.BlockSpec(memory_space=pltpu.VMEM)
    anywhere = pl.BlockSpec(memory_space=pl.ANY)
    dma = pltpu.SemaphoreType.DMA
    power = pl.pallas_call(
        functools.partial(kernel, members, lax.axis_size("tm")),
        out_shape=jax.ShapeDtypeStruct((kept, BINS), jnp.float32),
        in_specs=[anywhere] * 3 + [vmem] * 5,
        out_specs=vmem,
        scratch_shapes=[
            pltpu.VMEM((own_len, width), jnp.bfloat16),
            pltpu.VMEM(time.shape, jnp.bfloat16),
            pltpu.VMEM(channel.shape, jnp.bfloat16),
            pltpu.VMEM((width // LANES, SHARED, LANES), jnp.bfloat16),
            pltpu.VMEM((TAPS, width), jnp.bfloat16),
            pltpu.VMEM((2 * TAPS, width), jnp.float32),
            pltpu.VMEM((2 * BINS, width), jnp.float32),
            pltpu.VMEM((2 * BINS, width), jnp.float32),
            pltpu.VMEM((2 * BINS, LANES), jnp.float32),
            pltpu.VMEM((slabs, members, 2, bins, LANES), jnp.bfloat16),
            pltpu.VMEM((slabs, members, 2, bins, LANES), jnp.bfloat16),
            pltpu.VMEM((bins, 2 * SHARED, DMS), jnp.bfloat16),
            pltpu.VMEM((RADIX, INNER, SHARED), jnp.bfloat16),
            pltpu.VMEM((RADIX * bins, 2 * INNER), jnp.float32),
            pltpu.VMEM((members, kept, bins), jnp.float32),
            pltpu.VMEM((members, kept, bins), jnp.float32),
            dma((3,)), dma((1 + slabs,)), dma((1 + slabs,)),
            dma((slabs, members)), dma((slabs, members)), dma((members,)), dma((members,)),
        ],
        compiler_params=pltpu.CompilerParams(
            vmem_limit_bytes=56 * 2**20, collective_id=0, has_side_effects=True
        ),
    )(raw_samples, time, channel, filter_taps, units, dm_trials.reshape(1, DMS), tap, twiddle)
    return power[None]


def solution(mesh):
    in_specs = (P(("beam", "tm"), "freq"), P(None, "freq"), P(), P())
    out_specs = P(("beam", "tm"), "freq", None)
    return jax.shard_map(body, mesh=mesh, in_specs=in_specs, out_specs=out_specs, check_vma=False)
```
